256 devices in a mesh: seq: 32 (over x, y, core), ch: 8 (over z).
Axes of the slice: x: 4, y: 4, z: 8, core: 2. Of those that a mesh axis runs over, the one named last changes fastest.
Arguments:
- signal: bfloat16 [128, 16384], P('ch', 'seq'), may hold values from -6 to 6
- cotangent: bfloat16 [128, 16384], P('ch', 'seq'), may hold values from -6 to 6
- filter_taps: float32 [16, 16384], P(None, 'seq'), may hold values from -0.046875 to 0.046875
- skip_gain: float32 [128], P('ch'), may hold values from 0.5 to 1.5
Outputs:
- output: bfloat16 [128, 16384], P('ch', 'seq')
- input_grad: bfloat16 [128, 16384], P('ch', 'seq')
- grad_filter: float32 [16, 16384], P('ch', 'seq')
- grad_skip: float32 [128], replicated
The draws below stay inside these ranges and needn't reach their ends.
All inputs are finite; a program needn't handle non-finite values.
Results may differ from the reference program's by a relative error of at most 0.0012.
Values sent between devices are 32-bit elements; how exact they have to be, the bound alone decides.
A program may use at most 64 MiB of HBM per device.

```python
import math
import jax
import jax.numpy as jnp
from jax import lax

CH = 128
NFILT = 16
SEQ = 16384


def shard_levels(stream_key, dims, cuts, low, top_value):
    level = 1.0
    for axis_at, parts in cuts:
        heights = jax.random.uniform(jax.random.fold_in(jax.random.fold_in(stream_key, 6), axis_at), (parts,), jnp.float32, low / len(cuts), top_value / len(cuts))
        level = level * jnp.repeat(jnp.exp(heights), dims[axis_at] // parts).reshape((-1,) + (1,) * (len(dims) - 1 - axis_at))
    return level


def gaussian(stream_key, extent, scale, bound, shards=(), kind=jnp.bfloat16):
    loudness = shard_levels(stream_key, extent, shards, -0.22, 0.18) if shards else 1.0
    result = jax.random.normal(stream_key, extent, jnp.float32) * scale * loudness
    return jnp.minimum(jnp.maximum(result, -bound), bound).astype(kind)


def setup_inputs(seed: int = 0) -> dict:
    splits = jax.random.split(jax.random.key(seed), 5)
    signal = gaussian(splits[0], (CH, SEQ), 1.0, 6.0, ((0, 8), (1, 32)))
    cotangent = gaussian(splits[1], (CH, SEQ), 1.0, 6.0, ((0, 8), (1, 32)))
    filter_taps = gaussian(splits[2], (NFILT, SEQ), SEQ ** -0.5, 0.046875, ((1, 32),), jnp.float32)
    skip_gain = jnp.clip(1.0 + 0.1 * jax.random.normal(splits[3], (CH,), jnp.float32), 0.5, 1.5)
    return {"signal": signal, "cotangent": cotangent, "filter_taps": filter_taps, "skip_gain": skip_gain}


def reference(signal, cotangent, filter_taps, skip_gain):
    length = 2 * SEQ
    signal_f = signal.astype(jnp.float32)
    cot_f = cotangent.astype(jnp.float32)
    chan_filters = filter_taps[jnp.arange(CH) % NFILT]
    signal_spec = jnp.fft.rfft(signal_f, n=length, axis=1)
    cot_spec = jnp.fft.rfft(cot_f, n=length, axis=1)
    filter_spec = jnp.fft.rfft(chan_filters, n=length, axis=1)
    conv_out = jnp.fft.irfft(filter_spec * signal_spec, n=length, axis=1)[:, :SEQ]
    conv_grad = jnp.fft.irfft(jnp.conj(filter_spec) * cot_spec, n=length, axis=1)[:, :SEQ]
    output = (conv_out + skip_gain[:, None] * signal_f).astype(jnp.bfloat16)
    input_grad = (conv_grad + skip_gain[:, None] * cot_f).astype(jnp.bfloat16)
    cross_spec = jnp.conj(signal_spec) * cot_spec
    grouped = cross_spec.reshape(CH // NFILT, NFILT, cross_spec.shape[1]).sum(axis=0)
    lag_grad = jnp.fft.irfft(grouped, n=length, axis=1)[:, :SEQ]
    norm_scale = 1.0 / math.sqrt(SEQ)
    grad_filter = lag_grad * norm_scale
    grad_skip = lax.optimization_barrier(jnp.sum(cot_f * signal_f, axis=1)) * norm_scale
    return (output, input_grad, grad_filter, grad_skip)
```

```python
import functools
import math

import jax
import jax.numpy as jnp
import ml_dtypes
import numpy as np
from jax import lax
from jax.experimental import pallas as pl
from jax.experimental.pallas import tpu as pltpu
from jax.sharding import PartitionSpec as P

MESH = pl.DeviceIdType.MESH
F32, BF16 = jnp.float32, jnp.bfloat16

CHIPS = 16
PEERS = 32
DEPTH = 8
SIDE = 128
LENGTH = SIDE * SIDE
LOCAL = 512
PIECES = LOCAL // SIDE


def split(table):
    high = table.astype(ml_dtypes.bfloat16)
    low = (table - high.astype(np.float64)).astype(ml_dtypes.bfloat16)
    return high, low


@functools.cache
def tables():
    index = np.arange(SIDE)
    row = np.arange(SIDE)
    position = PIECES * (row % PEERS) + row // PEERS
    turn = 2.0 * np.pi * np.mod(np.outer(4 * index + 1, position), 4 * SIDE) / (4 * SIDE)
    first = np.concatenate([np.cos(turn), -np.sin(turn)], axis=0)
    first_high, first_low = split(first)
    small = 2.0 * np.pi * np.mod(np.outer(index, index), SIDE) / SIDE
    cosine, sine = np.cos(small), np.sin(small)
    middle = np.block([[cosine, -sine], [sine, cosine]])
    last = np.concatenate([np.cos(turn.T), -np.sin(turn.T)], axis=1) / LENGTH
    square = np.concatenate(
        [np.concatenate([first_high, first_low], axis=1), *split(middle), *split(middle.T), *split(last)],
        axis=0,
    )
    angle = 2.0 * np.pi * np.mod(np.outer(4 * index + 1, index), 4 * LENGTH) / (4 * LENGTH)
    twiddle = np.concatenate([np.cos(angle), np.sin(angle)], axis=0).astype(np.float32)
    return square, twiddle


FIRST, MID_H, MID_L, INV_H, INV_L, LAST_H, LAST_L = 0, 256, 512, 768, 1024, 1280, 1408
TABLE_ROWS = 1536


def dot(left, right):
    return jnp.dot(left, right, preferred_element_type=F32)


def halves(value):
    high = value.astype(BF16)
    return high, (value - high.astype(F32)).astype(BF16)


def dot_right(value, table_high, table_low):
    high, low = halves(value)
    return dot(high, table_high) + (dot(low, table_high) + dot(high, table_low))


def dot_left(table_high, table_low, value):
    high, low = halves(value)
    return dot(table_high, high) + (dot(table_high, low) + dot(table_low, high))


def twist(value, twiddle):
    cosine, sine = twiddle[0:SIDE], twiddle[SIDE:]
    real, imag = value[0:SIDE], value[SIDE:]
    return jnp.concatenate([real * cosine + imag * sine, imag * cosine - real * sine], axis=1)


def untwist(value, twiddle):
    cosine, sine = twiddle[0:SIDE], twiddle[SIDE:]
    real, imag = value[:, 0:SIDE], value[:, SIDE:]
    return jnp.concatenate([real * cosine - imag * sine, imag * cosine + real * sine], axis=0)


def forward_exact(value, table, twiddle):
    high = value.astype(BF16)
    columns = dot(table[FIRST : FIRST + 256], jnp.concatenate([high, high], axis=0))
    return twist(columns, twiddle)


def forward_full(value, table, twiddle):
    high, low = halves(value)
    columns = dot(table[FIRST : FIRST + 256], jnp.concatenate([high, high], axis=0))
    columns = columns + dot(table[FIRST : FIRST + 256, 0:SIDE], low)
    return twist(columns, twiddle)


def second(value, table):
    return dot_right(value, table[MID_H : MID_H + 256], table[MID_L : MID_L + 256])


def inverse(spectrum, table, twiddle):
    columns = dot_right(spectrum, table[INV_H : INV_H + 256], table[INV_L : INV_L + 256])
    return dot_left(
        table[LAST_H : LAST_H + SIDE], table[LAST_L : LAST_L + SIDE], untwist(columns, twiddle)
    )


def product(left, right):
    a, b, c, d = left[:, :SIDE], left[:, SIDE:], right[:, :SIDE], right[:, SIDE:]
    return jnp.concatenate([a * c - b * d, a * d + b * c], axis=1)


def product_conj(left, right):
    a, b, c, d = left[:, :SIDE], left[:, SIDE:], right[:, :SIDE], right[:, SIDE:]
    return jnp.concatenate([a * c + b * d, a * d - b * c], axis=1)


def kernel(
    sig_any, cot_any, taps_any, gain_any, table_any, twiddle_any,
    out_ref, grad_ref, lag_ref, skip_ref,
    sig, cot, taps, gain, table, twiddle,
    send_buf, recv_buf, back_buf, home_buf, lag_buf, lag_parts, lag_sum, lag_home, skip_row, skip_parts,
    local_sem, send_sem, recv_sem,
):
    me = lax.axis_index("seq")
    plane = lax.axis_index("ch")
    chip = me // 2
    is_owner = me % 2 == 0

    loads = [
        pltpu.make_async_copy(source, target, local_sem.at[i])
        for i, (source, target) in enumerate(
            ((sig_any, sig), (cot_any, cot), (taps_any, taps), (gain_any, gain), (table_any, table), (twiddle_any, twiddle))
        )
    ]
    for load in loads:
        load.start()

    barrier = pltpu.get_barrier_semaphore()

    def greet(seq, ch):
        pl.semaphore_signal(barrier, inc=1, device_id=(seq, ch), device_id_type=MESH)

    lag_plane = me // 4
    home_plane = chip // 2

    for i in range(1, CHIPS):
        greet(2 * ((chip + i) % CHIPS), plane)
    for j in range(2):
        source = 2 * (2 * plane + j)

        @pl.when(jnp.logical_or(source != me, lag_plane != plane))
        def _():
            greet(source, lag_plane)

    @pl.when(is_owner)
    def _():
        for i in range(CHIPS):
            greet(2 * ((chip + i) % CHIPS) + 1, plane)
        for i in range(1, DEPTH):
            greet(me, (plane + i) % DEPTH)

    @pl.when(jnp.logical_not(is_owner))
    def _():
        greet(me - 1, plane)

    for load in loads[:3]:
        load.wait()
    for r in range(PIECES):
        lanes = slice(SIDE * r, SIDE * (r + 1))
        send_buf[pl.ds(r, CHIPS, stride=16), :] = sig[:, lanes].astype(F32)
        send_buf[pl.ds(PIECES + r, CHIPS, stride=16), :] = cot[:, lanes].astype(F32)
        send_buf[pl.ds(2 * PIECES + r, CHIPS, stride=16), :] = taps[:, lanes]

    def slab(buf, index):
        return buf.at[pl.ds(pl.multiple_of(index * 16, 16), 16)]

    def remote(source, target, which, seq, ch):
        return pltpu.make_async_remote_copy(
            src_ref=source, dst_ref=target, send_sem=send_sem.at[which], recv_sem=recv_sem.at[which],
            device_id=(seq, ch), device_id_type=MESH,
        )

    def send_row(q):
        remote(slab(send_buf, q), slab(recv_buf, me), 0, 2 * q, plane).start()

    def wait_send(buf, slabs, which):
        view = buf.at[pl.ds(0, 16 * slabs)]
        pltpu.make_async_copy(view, view, send_sem.at[which]).wait()

    def wait_recv(buf, slabs, which):
        view = buf.at[pl.ds(0, 16 * slabs)]
        pltpu.make_async_copy(view, view, recv_sem.at[which]).wait()

    lag_self = jnp.logical_and(is_owner, home_plane == plane)

    @pl.when(jnp.logical_not(is_owner))
    def _():
        pl.semaphore_wait(barrier, CHIPS)
        for i in range(CHIPS):
            send_row((chip + i) % CHIPS)
        wait_recv(home_buf, CHIPS, 1)
        wait_send(send_buf, CHIPS, 0)
        for load in loads[3:]:
            load.wait()

    @pl.when(is_owner)
    def _():
        others = jnp.where(home_plane == plane, PIECES - 1, PIECES)
        pl.semaphore_wait(barrier, PEERS - 1 + DEPTH - 1 + others)
        for i in range(1, CHIPS):
            send_row((chip + i) % CHIPS)
        slab(recv_buf, me)[...] = slab(send_buf, chip)[...]
        for load in loads[3:]:
            load.wait()
        wait_recv(recv_buf, PEERS - 1, 0)

        def gather(part):
            return jnp.concatenate(
                [recv_buf[pl.ds(PIECES * part + r, PEERS, stride=16), :] for r in range(PIECES)], axis=0
            )

        signal, cotangent = gather(0), gather(1)
        row = jnp.sum(jnp.sum(signal * cotangent, axis=0, keepdims=True), axis=1, keepdims=True)
        lane = lax.broadcasted_iota(jnp.int32, (8, SIDE), 1)
        skip_row[...] = jnp.where(lane == plane * CHIPS + chip, row, 0.0)
        for i in range(1, DEPTH):
            there = (plane + i) % DEPTH
            remote(skip_row, skip_parts.at[plane], 2, me, there).start()

        signal_spec = second(forward_exact(signal, table, twiddle), table)
        cot_spec = second(forward_exact(cotangent, table, twiddle), table)
        lags = inverse(product_conj(signal_spec, cot_spec), table, twiddle)
        for r in range(PIECES):
            lag_buf[pl.ds(r, PEERS, stride=PIECES), :] = lags[PEERS * r : PEERS * (r + 1)]
        for i in range(1, DEPTH):
            there = (plane + i) % DEPTH
            remote(slab(lag_buf, there), lag_parts.at[plane], 3, me, there).start()
        lag_parts[plane] = slab(lag_buf, plane)[...]

        filter_spec = second(forward_full(gather(2), table, twiddle), table)
        own_gain = gain[chip]
        conv_out = inverse(product(filter_spec, signal_spec), table, twiddle) + own_gain * signal
        conv_grad = inverse(product_conj(filter_spec, cot_spec), table, twiddle) + own_gain * cotangent
        for r in range(PIECES):
            rows = slice(PEERS * r, PEERS * (r + 1))
            back_buf[pl.ds(r, PEERS, stride=16), :] = conv_out[rows]
            back_buf[pl.ds(PIECES + r, PEERS, stride=16), :] = conv_grad[rows]

        skip_view = skip_parts.at[pl.ds(0, DEPTH - 1)]
        pltpu.make_async_copy(skip_view, skip_view, recv_sem.at[2]).wait()
        skip_parts[plane] = skip_row[...]
        skip_all = jnp.sum(skip_parts[...], axis=0)[0:1]
        back_buf[pl.ds(8, PEERS, stride=16), :] = jnp.broadcast_to(skip_all, (PEERS, SIDE))

        for i in range(1, PEERS):
            there = (me + i) % PEERS
            remote(slab(back_buf, there), slab(home_buf, chip), 1, there, plane).start()
        slab(home_buf, chip)[...] = slab(back_buf, me)[...]

        part_view = lag_parts.at[pl.ds(0, DEPTH - 1)]
        pltpu.make_async_copy(part_view, part_view, recv_sem.at[3]).wait()
        total = jnp.sum(lag_parts[...], axis=0) * (1.0 / math.sqrt(LENGTH))
        for j in range(PIECES):
            lag_sum[j, 0:PIECES] = total[PIECES * j : PIECES * (j + 1)]
        for j in range(PIECES):
            there = PIECES * plane + j
            same = jnp.logical_and(there == me, home_plane == plane)

            @pl.when(jnp.logical_not(same))
            def _():
                remote(lag_sum.at[j], lag_home.at[chip % 2], 4 + chip % 2, there, home_plane).start()

            @pl.when(same)
            def _():
                lag_home[chip % 2] = lag_sum[j]

        wait_recv(home_buf, CHIPS - 1, 1)
        wait_send(send_buf, CHIPS - 1, 0)
        wait_send(back_buf, PEERS - 1, 1)
        pltpu.make_async_copy(skip_view, skip_view, send_sem.at[2]).wait()
        pltpu.make_async_copy(part_view, part_view, send_sem.at[3]).wait()

        @pl.when(lag_self)
        def _():
            view = lag_sum.at[pl.ds(0, PIECES - 1)]
            pltpu.make_async_copy(view, view, send_sem.at[4 + chip % 2]).wait()

        @pl.when(jnp.logical_not(lag_self))
        def _():
            pltpu.make_async_copy(lag_sum, lag_sum, send_sem.at[4 + chip % 2]).wait()

    for j in range(2):

        @pl.when(jnp.logical_or(2 * (2 * plane + j) != me, lag_plane != plane))
        def _():
            view = lag_home.at[j]
            pltpu.make_async_copy(view, view, recv_sem.at[4 + j]).wait()

    for r in range(PIECES):
        lanes = slice(SIDE * r, SIDE * (r + 1))
        out_ref[:, lanes] = home_buf[pl.ds(r, CHIPS, stride=16), :].astype(BF16)
        grad_ref[:, lanes] = home_buf[pl.ds(PIECES + r, CHIPS, stride=16), :].astype(BF16)
        for j in range(2):
            lag_ref[j : j + 1, lanes] = lag_home[j, r : r + 1]
    skip_ref[...] = jnp.sum(home_buf[pl.ds(8, CHIPS, stride=16), :], axis=0, keepdims=True) * (1.0 / math.sqrt(LENGTH))


def on_device(signal, cotangent, filter_taps, skip_gain):
    square, twiddle = tables()
    anywhere = pl.BlockSpec(memory_space=pl.ANY)
    vmem = pl.BlockSpec(memory_space=pltpu.VMEM)
    out, grad, lag, skip = pl.pallas_call(
        kernel,
        out_shape=(
            jax.ShapeDtypeStruct((CHIPS, LOCAL), BF16),
            jax.ShapeDtypeStruct((CHIPS, LOCAL), BF16),
            jax.ShapeDtypeStruct((2, LOCAL), F32),
            jax.ShapeDtypeStruct((1, SIDE), F32),
        ),
        in_specs=[anywhere] * 6,
        out_specs=(vmem,) * 4,
        scratch_shapes=[
            pltpu.VMEM((CHIPS, LOCAL), BF16),
            pltpu.VMEM((CHIPS, LOCAL), BF16),
            pltpu.VMEM((CHIPS, LOCAL), F32),
            pltpu.SMEM((CHIPS,), F32),
            pltpu.VMEM((TABLE_ROWS, 2 * SIDE), BF16),
            pltpu.VMEM((2 * SIDE, SIDE), F32),
            pltpu.VMEM((CHIPS * 16, SIDE), F32),
            pltpu.VMEM((PEERS * 16, SIDE), F32),
            pltpu.VMEM((PEERS * 16, SIDE), F32),
            pltpu.VMEM((CHIPS * 16, SIDE), F32),
            pltpu.VMEM((SIDE, SIDE), F32),
            pltpu.VMEM((DEPTH, 16, SIDE), F32),
            pltpu.VMEM((PIECES, 8, SIDE), F32),
            pltpu.VMEM((2, 8, SIDE), F32),
            pltpu.VMEM((8, SIDE), F32),
            pltpu.VMEM((DEPTH, 8, SIDE), F32),
            pltpu.SemaphoreType.DMA((6,)),
            pltpu.SemaphoreType.DMA((6,)),
            pltpu.SemaphoreType.DMA((6,)),
        ],
        compiler_params=pltpu.CompilerParams(
            collective_id=0, has_side_effects=True, vmem_limit_bytes=32 * 1024 * 1024
        ),
    )(signal, cotangent, filter_taps, skip_gain, jnp.asarray(square), jnp.asarray(twiddle))
    return out, grad, lag, skip.reshape(SIDE)


def solution(mesh):
    in_specs = (P("ch", "seq"), P("ch", "seq"), P(None, "seq"), P("ch"))
    out_specs = (P("ch", "seq"), P("ch", "seq"), P("ch", "seq"), P())
    return jax.shard_map(on_device, mesh=mesh, in_specs=in_specs, out_specs=out_specs, check_vma=False)
```

```python
import functools
import math

import jax
import jax.numpy as jnp
import ml_dtypes
import numpy as np
from jax import lax
from jax.experimental import pallas as pl
from jax.experimental.pallas import tpu as pltpu
from jax.sharding import PartitionSpec as P

MESH = pl.DeviceIdType.MESH
F32, BF16 = jnp.float32, jnp.bfloat16

CHIPS = 16
PEERS = 32
DEPTH = 8
SIDE = 128
LENGTH = SIDE * SIDE
LOCAL = 512
PIECES = LOCAL // SIDE
SCALE = 1.0 / math.sqrt(LENGTH)


def hops(mask):
    return (0, 1, 2, 1)[mask & 3]


CHIP_MASKS = sorted(range(1, CHIPS), key=lambda m: -hops(m) - hops(m >> 2))
DEPTH_STEPS = sorted(range(1, DEPTH), key=lambda i: -min(i, DEPTH - i))


def split(table):
    high = table.astype(ml_dtypes.bfloat16)
    low = (table - high.astype(np.float64)).astype(ml_dtypes.bfloat16)
    return high, low


@functools.cache
def tables():
    index = np.arange(SIDE)
    row = np.arange(SIDE)
    position = PIECES * (row % PEERS) + row // PEERS
    turn = 2.0 * np.pi * np.mod(np.outer(4 * index + 1, position), 4 * SIDE) / (4 * SIDE)
    first = np.concatenate([np.cos(turn), -np.sin(turn)], axis=0)
    first_high, first_low = split(first)
    small = 2.0 * np.pi * np.mod(np.outer(index, index), SIDE) / SIDE
    cosine, sine = np.cos(small), np.sin(small)
    middle = np.block([[cosine, -sine], [sine, cosine]])
    last = np.concatenate([np.cos(turn.T), -np.sin(turn.T)], axis=1) / LENGTH
    square = np.concatenate(
        [np.concatenate([first_high, first_low], axis=1), *split(middle), *split(middle.T), *split(last)],
        axis=0,
    )
    angle = 2.0 * np.pi * np.mod(np.outer(4 * index + 1, index), 4 * LENGTH) / (4 * LENGTH)
    twiddle = np.concatenate([np.cos(angle), np.sin(angle)], axis=0).astype(np.float32)
    return square, twiddle


FIRST, MID_H, MID_L, INV_H, INV_L, LAST_H, LAST_L = 0, 256, 512, 768, 1024, 1280, 1408
TABLE_ROWS = 1536


def dot(left, right):
    return jnp.dot(left, right, preferred_element_type=F32)


def halves(value):
    high = value.astype(BF16)
    return high, (value - high.astype(F32)).astype(BF16)


def dot_right(value, table_high, table_low):
    high, low = halves(value)
    return dot(high, table_high) + (dot(low, table_high) + dot(high, table_low))


def dot_left(table_high, table_low, value):
    high, low = halves(value)
    return dot(table_high, high) + (dot(table_high, low) + dot(table_low, high))


def twist(value, twiddle):
    cosine, sine = twiddle[0:SIDE], twiddle[SIDE:]
    real, imag = value[0:SIDE], value[SIDE:]
    return jnp.concatenate([real * cosine + imag * sine, imag * cosine - real * sine], axis=1)


def untwist(value, twiddle):
    cosine, sine = twiddle[0:SIDE], twiddle[SIDE:]
    real, imag = value[:, 0:SIDE], value[:, SIDE:]
    return jnp.concatenate([real * cosine - imag * sine, imag * cosine + real * sine], axis=0)


def forward_exact(value, table, twiddle):
    high = value.astype(BF16)
    columns = dot(table[FIRST : FIRST + 256], jnp.concatenate([high, high], axis=0))
    return twist(columns, twiddle)


def forward_full(value, table, twiddle):
    high, low = halves(value)
    columns = dot(table[FIRST : FIRST + 256], jnp.concatenate([high, high], axis=0))
    columns = columns + dot(table[FIRST : FIRST + 256, 0:SIDE], low)
    return twist(columns, twiddle)


def second(value, table):
    return dot_right(value, table[MID_H : MID_H + 256], table[MID_L : MID_L + 256])


def inverse(spectrum, table, twiddle):
    columns = dot_right(spectrum, table[INV_H : INV_H + 256], table[INV_L : INV_L + 256])
    return dot_left(
        table[LAST_H : LAST_H + SIDE], table[LAST_L : LAST_L + SIDE], untwist(columns, twiddle)
    )


def product(left, right):
    a, b, c, d = left[:, :SIDE], left[:, SIDE:], right[:, :SIDE], right[:, SIDE:]
    return jnp.concatenate([a * c - b * d, a * d + b * c], axis=1)


def product_conj(left, right):
    a, b, c, d = left[:, :SIDE], left[:, SIDE:], right[:, :SIDE], right[:, SIDE:]
    return jnp.concatenate([a * c + b * d, a * d - b * c], axis=1)


def exchange(
    sig_any, cot_any, taps_any, gain_any, table_any, twiddle_any,
    home_buf, lag_home,
    sig, cot, taps, gain, table, twiddle,
    send_buf, recv_buf, back_buf, lag_buf, skip_row, skip_pair, skip_parts,
    local_sem, send_sem, recv_sem, ready_sem,
):
    me = lax.axis_index("seq")
    plane = lax.axis_index("ch")
    chip = me // 2
    is_owner = me % 2 == 0
    not_owner = jnp.logical_not(is_owner)
    lag_plane = chip // 2
    in_place = lag_plane == plane

    loads = [
        pltpu.make_async_copy(source, target, local_sem.at[i])
        for i, (source, target) in enumerate(
            ((sig_any, sig), (cot_any, cot), (taps_any, taps), (gain_any, gain), (table_any, table), (twiddle_any, twiddle))
        )
    ]
    for load in loads[:3]:
        load.start()

    barrier = pltpu.get_barrier_semaphore()

    def greet(seq, ch):
        pl.semaphore_signal(barrier, inc=1, device_id=(seq, ch), device_id_type=MESH)

    @pl.when(is_owner)
    def _():
        for i in DEPTH_STEPS:
            greet(me, (plane + i) % DEPTH)
        for mask in CHIP_MASKS:
            greet(me ^ (2 * mask), plane)
            greet(me ^ (2 * mask + 1), plane)
        greet(me ^ 1, plane)
        for load in loads[3:]:
            load.start()

    @pl.when(not_owner)
    def _():
        for mask in CHIP_MASKS:
            greet(me ^ (2 * mask + 1), plane)
        greet(me ^ 1, plane)

    for load in loads[:3]:
        load.wait()
    for r in range(PIECES):
        lanes = slice(SIDE * r, SIDE * (r + 1))
        send_buf[pl.ds(r, CHIPS, stride=16), :] = sig[:, lanes].astype(F32)
        send_buf[pl.ds(PIECES + r, CHIPS, stride=16), :] = cot[:, lanes].astype(F32)
        send_buf[pl.ds(2 * PIECES + r, CHIPS, stride=16), :] = taps[:, lanes]
    share = jnp.sum(sig[...].astype(F32) * cot[...].astype(F32), axis=1, keepdims=True)
    lane = lax.broadcasted_iota(jnp.int32, (CHIPS, SIDE), 1)
    local = lax.broadcasted_iota(jnp.int32, (CHIPS, SIDE), 0)
    share = jnp.sum(jnp.where(lane == plane * CHIPS + local, share, 0.0), axis=0, keepdims=True)
    skip_row[...] = jnp.broadcast_to(share, (8, SIDE))

    def slab(buf, index, rows):
        return buf.at[pl.ds(pl.multiple_of(index * 16, 16), rows)]

    def remote(source, target, which, seq, ch):
        return pltpu.make_async_remote_copy(
            src_ref=source, dst_ref=target, send_sem=send_sem.at[which], recv_sem=recv_sem.at[which],
            device_id=(seq, ch), device_id_type=MESH,
        )

    def wait_for(view, sem):
        pltpu.make_async_copy(view, view, sem).wait()

    def send_inputs(mask):
        q = chip ^ mask
        remote(slab(send_buf, q, 16), slab(recv_buf, me, 16), 0, 2 * q, plane).start()

    home_rows = 16

    @pl.when(not_owner)
    def _():
        pl.semaphore_wait(barrier, CHIPS)
        for mask in CHIP_MASKS:
            send_inputs(mask)
        send_inputs(0)
        pair = remote(skip_row, skip_pair, 2, me ^ 1, plane)
        pair.start()
        wait_for(send_buf, send_sem.at[0])
        pair.wait_send()
        wait_for(home_buf, recv_sem.at[1])

    @pl.when(is_owner)
    def _():
        pl.semaphore_wait(barrier, PEERS - 1 + DEPTH - 1)
        for mask in CHIP_MASKS:
            send_inputs(mask)

        @pl.when(in_place)
        def _():
            for i in DEPTH_STEPS:
                pl.semaphore_signal(
                    ready_sem, inc=1, device_id=(me, (plane + i) % DEPTH), device_id_type=MESH
                )

        slab(recv_buf, me, 16)[...] = slab(send_buf, chip, 16)[...]
        remote(skip_row, skip_pair, 2, me, plane).wait_recv()
        skip_row[...] = skip_row[...] + skip_pair[...]
        for i in DEPTH_STEPS:
            remote(skip_row, skip_parts.at[plane], 3, me, (plane + i) % DEPTH).start()
        skip_parts[plane] = skip_row[...]
        for load in loads[3:]:
            load.wait()
        wait_for(recv_buf.at[pl.ds(0, 16 * (PEERS - 1))], recv_sem.at[0])

        def gather(part):
            return jnp.concatenate(
                [recv_buf[pl.ds(PIECES * part + r, PEERS, stride=16), :] for r in range(PIECES)], axis=0
            )

        signal, cotangent = gather(0), gather(1)
        signal_spec = second(forward_exact(signal, table, twiddle), table)
        cot_spec = second(forward_exact(cotangent, table, twiddle), table)
        lags = inverse(product_conj(signal_spec, cot_spec), table, twiddle)
        for r in range(PIECES):
            lag_buf[:, r, :] = lags[PEERS * r : PEERS * (r + 1)]

        @pl.when(jnp.logical_not(in_place))
        def _():
            pl.semaphore_wait(ready_sem, 1)

        slot = (chip % 2) * DEPTH + plane

        def send_lags(mask):
            there = me ^ mask
            return remote(lag_buf.at[there], lag_home.at[slot], 4, there, lag_plane)

        for mask in CHIP_MASKS:
            send_lags(2 * mask).start()
            send_lags(2 * mask + 1).start()
        send_lags(1).start()

        @pl.when(in_place)
        def _():
            pltpu.make_async_copy(lag_buf.at[me], lag_home.at[slot], recv_sem.at[4]).start()

        @pl.when(jnp.logical_not(in_place))
        def _():
            send_lags(0).start()

        filter_spec = second(forward_full(gather(2), table, twiddle), table)
        own_gain = gain[chip]
        conv_out = inverse(product(filter_spec, signal_spec), table, twiddle) + own_gain * signal
        conv_grad = inverse(product_conj(filter_spec, cot_spec), table, twiddle) + own_gain * cotangent
        for r in range(PIECES):
            rows = slice(PEERS * r, PEERS * (r + 1))
            back_buf[pl.ds(r, PEERS, stride=16), :] = conv_out[rows]
            back_buf[pl.ds(PIECES + r, PEERS, stride=16), :] = conv_grad[rows]

        skip_view = skip_parts.at[pl.ds(0, DEPTH - 1)]
        wait_for(skip_view, recv_sem.at[3])
        skip_all = jnp.sum(skip_parts[...], axis=0)[0:1]
        back_buf[pl.ds(8, PEERS, stride=16), :] = jnp.broadcast_to(skip_all, (PEERS, SIDE))

        def send_results(mask):
            there = me ^ mask
            remote(slab(back_buf, there, home_rows), slab(home_buf, chip, home_rows), 1, there, plane).start()

        for mask in CHIP_MASKS:
            send_results(2 * mask)
            send_results(2 * mask + 1)
        send_results(1)
        slab(home_buf, chip, 16)[...] = slab(back_buf, me, 16)[...]

        wait_for(send_buf.at[pl.ds(0, 16 * (CHIPS - 1))], send_sem.at[0])
        wait_for(skip_view, send_sem.at[3])
        wait_for(lag_buf.at[pl.ds(0, PEERS - 1)], send_sem.at[4])

        @pl.when(jnp.logical_not(in_place))
        def _():
            wait_for(lag_buf.at[0], send_sem.at[4])

        wait_for(back_buf.at[pl.ds(0, home_rows * (PEERS - 1))], send_sem.at[1])
        wait_for(home_buf.at[pl.ds(0, home_rows * (CHIPS - 1))], recv_sem.at[1])

    wait_for(lag_home, recv_sem.at[4])


def finish(home_buf, lag_home, out_ref, grad_ref, lag_ref, skip_ref):
    for r in range(PIECES):
        lanes = slice(SIDE * r, SIDE * (r + 1))
        out_ref[:, lanes] = home_buf[pl.ds(r, CHIPS, stride=16), :].astype(BF16)
        grad_ref[:, lanes] = home_buf[pl.ds(PIECES + r, CHIPS, stride=16), :].astype(BF16)
    for j in range(2):
        lags = jnp.sum(lag_home[DEPTH * j : DEPTH * (j + 1)], axis=0) * SCALE
        for r in range(PIECES):
            lag_ref[j : j + 1, SIDE * r : SIDE * (r + 1)] = lags[r : r + 1]
    skip_ref[...] = jnp.sum(home_buf[pl.ds(8, CHIPS, stride=16), :], axis=0) * SCALE


def on_device(signal, cotangent, filter_taps, skip_gain):
    square, twiddle = tables()
    anywhere = pl.BlockSpec(memory_space=pl.ANY)
    vmem = pl.BlockSpec(memory_space=pltpu.VMEM)
    operands = (signal, cotangent, filter_taps, skip_gain, jnp.asarray(square), jnp.asarray(twiddle))
    home, lags = pl.pallas_call(
        exchange,
        out_shape=(
            pltpu.VMEM((CHIPS * 16, SIDE), F32),
            pltpu.VMEM((2 * DEPTH, PIECES, SIDE), F32),
        ),
        in_specs=[anywhere] * 6,
        out_specs=(vmem,) * 2,
        scratch_shapes=[
            pltpu.VMEM((CHIPS, LOCAL), BF16),
            pltpu.VMEM((CHIPS, LOCAL), BF16),
            pltpu.VMEM((CHIPS, LOCAL), F32),
            pltpu.SMEM((CHIPS,), F32),
            pltpu.VMEM((TABLE_ROWS, 2 * SIDE), BF16),
            pltpu.VMEM((2 * SIDE, SIDE), F32),
            pltpu.VMEM((CHIPS * 16, SIDE), F32),
            pltpu.VMEM((PEERS * 16, SIDE), F32),
            pltpu.VMEM((PEERS * 16, SIDE), F32),
            pltpu.VMEM((PEERS, PIECES, SIDE), F32),
            pltpu.VMEM((8, SIDE), F32),
            pltpu.VMEM((8, SIDE), F32),
            pltpu.VMEM((DEPTH, 8, SIDE), F32),
            pltpu.SemaphoreType.DMA((6,)),
            pltpu.SemaphoreType.DMA((5,)),
            pltpu.SemaphoreType.DMA((5,)),
            pltpu.SemaphoreType.REGULAR,
        ],
        compiler_params=pltpu.CompilerParams(
            collective_id=0, has_side_effects=True, vmem_limit_bytes=32 * 1024 * 1024
        ),
        name="exchange",
    )(*(pltpu.with_memory_space_constraint(operand, pltpu.HBM) for operand in operands))
    return pl.pallas_call(
        finish,
        out_shape=(
            jax.ShapeDtypeStruct((CHIPS, LOCAL), BF16),
            jax.ShapeDtypeStruct((CHIPS, LOCAL), BF16),
            jax.ShapeDtypeStruct((2, LOCAL), F32),
            jax.ShapeDtypeStruct((SIDE,), F32),
        ),
        in_specs=[vmem] * 2,
        out_specs=(vmem,) * 4,
        compiler_params=pltpu.CompilerParams(vmem_limit_bytes=8 * 1024 * 1024),
        name="finish",
    )(home, lags)


def solution(mesh):
    in_specs = (P("ch", "seq"), P("ch", "seq"), P(None, "seq"), P("ch"))
    out_specs = (P("ch", "seq"), P("ch", "seq"), P("ch", "seq"), P())
    return jax.shard_map(on_device, mesh=mesh, in_specs=in_specs, out_specs=out_specs, check_vma=False)
```

```python
import functools
import math

import jax
import jax.numpy as jnp
import ml_dtypes
import numpy as np
from jax import lax
from jax.experimental import pallas as pl
from jax.experimental.pallas import tpu as pltpu
from jax.sharding import PartitionSpec as P

MESH = pl.DeviceIdType.MESH
F32, BF16 = jnp.float32, jnp.bfloat16

CHIPS = 16
PEERS = 32
DEPTH = 8
SIDE = 128
LENGTH = SIDE * SIDE
LOCAL = 512
ROWS = 8
HUB = 1
PIECES = LOCAL // SIDE
SCALE = 1.0 / math.sqrt(LENGTH)


def hops(mask):
    return (0, 1, 2, 1)[mask & 3]


CHIP_MASKS = sorted(range(1, CHIPS), key=lambda m: -hops(m) - hops(m >> 2))
DEPTH_STEPS = sorted(range(1, DEPTH), key=lambda i: -min(i, DEPTH - i))


def split(table):
    high = table.astype(ml_dtypes.bfloat16)
    low = (table - high.astype(np.float64)).astype(ml_dtypes.bfloat16)
    return high, low


@functools.cache
def tables():
    index = np.arange(SIDE)
    row = np.arange(SIDE)
    position = PIECES * (row % PEERS) + row // PEERS
    turn = 2.0 * np.pi * np.mod(np.outer(4 * index + 1, position), 4 * SIDE) / (4 * SIDE)
    first = np.concatenate([np.cos(turn), -np.sin(turn)], axis=0)
    first_high, first_low = split(first)
    small = 2.0 * np.pi * np.mod(np.outer(index, index), SIDE) / SIDE
    cosine, sine = np.cos(small), np.sin(small)
    middle = np.block([[cosine, -sine], [sine, cosine]])
    last = np.concatenate([np.cos(turn.T), -np.sin(turn.T)], axis=1) / LENGTH
    square = np.concatenate(
        [np.concatenate([first_high, first_low], axis=1), *split(middle), *split(middle.T), *split(last)],
        axis=0,
    )
    angle = 2.0 * np.pi * np.mod(np.outer(4 * index + 1, index), 4 * LENGTH) / (4 * LENGTH)
    twiddle = np.concatenate([np.cos(angle), np.sin(angle)], axis=0).astype(np.float32)
    return square, twiddle


FIRST, MID_H, MID_L, INV_H, INV_L, LAST_H, LAST_L = 0, 256, 512, 768, 1024, 1280, 1408
TABLE_ROWS = 1536


def dot(left, right):
    return jnp.dot(left, right, preferred_element_type=F32)


def halves(value):
    high = value.astype(BF16)
    return high, (value - high.astype(F32)).astype(BF16)


def dot_right(value, table_high, table_low):
    high, low = halves(value)
    return dot(high, table_high) + (dot(low, table_high) + dot(high, table_low))


def dot_left(table_high, table_low, value):
    high, low = halves(value)
    return dot(table_high, high) + (dot(table_high, low) + dot(table_low, high))


def twist(value, twiddle):
    cosine, sine = twiddle[0:SIDE], twiddle[SIDE:]
    real, imag = value[0:SIDE], value[SIDE:]
    return jnp.concatenate([real * cosine + imag * sine, imag * cosine - real * sine], axis=1)


def untwist(value, twiddle):
    cosine, sine = twiddle[0:SIDE], twiddle[SIDE:]
    real, imag = value[:, 0:SIDE], value[:, SIDE:]
    return jnp.concatenate([real * cosine - imag * sine, imag * cosine + real * sine], axis=0)


def forward_exact(value, table, twiddle):
    high = value.astype(BF16)
    columns = dot(table[FIRST : FIRST + 256], jnp.concatenate([high, high], axis=0))
    return twist(columns, twiddle)


def forward_full(value, table, twiddle):
    high, low = halves(value)
    columns = dot(table[FIRST : FIRST + 256], jnp.concatenate([high, high], axis=0))
    columns = columns + dot(table[FIRST : FIRST + 256, 0:SIDE], low)
    return twist(columns, twiddle)


def second(value, table):
    return dot_right(value, table[MID_H : MID_H + 256], table[MID_L : MID_L + 256])


def inverse(spectrum, table, twiddle):
    columns = dot_right(spectrum, table[INV_H : INV_H + 256], table[INV_L : INV_L + 256])
    return dot_left(
        table[LAST_H : LAST_H + SIDE], table[LAST_L : LAST_L + SIDE], untwist(columns, twiddle)
    )


def product(left, right):
    a, b, c, d = left[:, :SIDE], left[:, SIDE:], right[:, :SIDE], right[:, SIDE:]
    return jnp.concatenate([a * c - b * d, a * d + b * c], axis=1)


def product_conj(left, right):
    a, b, c, d = left[:, :SIDE], left[:, SIDE:], right[:, :SIDE], right[:, SIDE:]
    return jnp.concatenate([a * c + b * d, a * d - b * c], axis=1)


def exchange(
    sig_any, cot_any, taps_any, gain_any, table_any, twiddle_any,
    home_buf, lag_home, skip_home,
    sig, cot, taps, gain, table, twiddle,
    send_buf, send_taps_buf, recv_buf, recv_taps_buf, back_buf, lag_buf, skip_row, skip_in, skip_sum, skip_parts,
    local_sem, send_sem, recv_sem, plane_sem, ready_sem,
):
    me = lax.axis_index("seq")
    plane = lax.axis_index("ch")
    chip = me // 2
    is_owner = me % 2 == 0
    is_hub = me == HUB
    shift = (PIECES - (plane & 6)) & 7

    def channel_of(p):
        return 2 * (((p >> 1) + shift) & 7) + (p & 1)

    channel = channel_of(chip)
    lag_plane = channel // 2
    in_place = lag_plane == plane

    loads = [
        pltpu.make_async_copy(source, target, local_sem.at[i])
        for i, (source, target) in enumerate(
            ((sig_any, sig), (cot_any, cot), (taps_any, taps), (gain_any, gain), (table_any, table), (twiddle_any, twiddle))
        )
    ]
    for load in loads[:3]:
        load.start()

    barrier = pltpu.get_barrier_semaphore()

    def greet(seq, ch):
        pl.semaphore_signal(barrier, inc=1, device_id=(seq, ch), device_id_type=MESH)

    @pl.when(jnp.logical_or(is_owner, is_hub))
    def _():
        for mask in CHIP_MASKS:
            greet(me ^ (2 * mask), plane)
            greet(me ^ (2 * mask + 1), plane)
        greet(me ^ 1, plane)

    @pl.when(is_hub)
    def _():
        for i in DEPTH_STEPS:
            greet(me, (plane + i) % DEPTH)

    @pl.when(is_owner)
    def _():
        for load in loads[3:]:
            load.start()

    @pl.when(jnp.logical_not(jnp.logical_or(is_owner, is_hub)))
    def _():
        for mask in CHIP_MASKS:
            greet(me ^ (2 * mask + 1), plane)
        greet(me ^ 1, plane)
        greet(HUB, plane)

    for load in loads[:2]:
        load.wait()
    share = jnp.sum(sig[...].astype(F32) * cot[...].astype(F32), axis=1, keepdims=True)
    lane = lax.broadcasted_iota(jnp.int32, (CHIPS, SIDE), 1)
    local = lax.broadcasted_iota(jnp.int32, (CHIPS, SIDE), 0)
    skip_row[...] = jnp.sum(jnp.where(lane == plane * CHIPS + local, share, 0.0), axis=0, keepdims=True)
    for r in range(PIECES):
        lanes = slice(SIDE * r, SIDE * (r + 1))
        send_buf[pl.ds(r, CHIPS, stride=ROWS), :] = sig[:, lanes].astype(F32)
        send_buf[pl.ds(PIECES + r, CHIPS, stride=ROWS), :] = cot[:, lanes].astype(F32)
    loads[2].wait()
    for r in range(PIECES):
        send_taps_buf[:, r, :] = taps[:, SIDE * r : SIDE * (r + 1)]

    def slab(buf, index):
        return buf.at[pl.ds(pl.multiple_of(index * ROWS, ROWS), ROWS)]

    def remote(source, target, which, seq, ch):
        return pltpu.make_async_remote_copy(
            src_ref=source, dst_ref=target, send_sem=send_sem.at[which], recv_sem=recv_sem.at[which],
            device_id=(seq, ch), device_id_type=MESH,
        )

    def wait_for(view, sem):
        pltpu.make_async_copy(view, view, sem).wait()

    def send_rows(mask):
        q = chip ^ mask
        remote(slab(send_buf, channel_of(q)), slab(recv_buf, me), 0, 2 * q, plane).start()

    def send_taps(mask):
        q = chip ^ mask
        remote(send_taps_buf.at[channel_of(q)], recv_taps_buf.at[me], 5, 2 * q, plane).start()

    def send_share():
        remote(skip_row, skip_in.at[me], 2, HUB, plane).start()

    def wait_skip():
        wait_for(skip_row, send_sem.at[2])
        wait_for(skip_home, recv_sem.at[6])

    @pl.when(jnp.logical_not(is_owner))
    def _():
        @pl.when(is_hub)
        def _():
            pl.semaphore_wait(barrier, PEERS - 1 + DEPTH - 1)
            for i in DEPTH_STEPS:
                pl.semaphore_signal(
                    plane_sem, inc=1, device_id=(me, (plane + i) % DEPTH), device_id_type=MESH
                )

        @pl.when(jnp.logical_not(is_hub))
        def _():
            pl.semaphore_wait(barrier, CHIPS + 1)
            send_share()

        for mask in (*CHIP_MASKS, 0):
            send_rows(mask)
        for mask in (*CHIP_MASKS, 0):
            send_taps(mask)

        @pl.when(is_hub)
        def _():
            pl.semaphore_wait(plane_sem, DEPTH - 1)
            for mask in (*CHIP_MASKS, 0):
                pl.semaphore_signal(
                    ready_sem, inc=1, device_id=(2 * (chip ^ mask), plane), device_id_type=MESH
                )
            wait_for(skip_in.at[pl.ds(0, PEERS - 1)], recv_sem.at[2])
            skip_in[me] = skip_row[...]
            skip_sum[...] = jnp.sum(skip_in[...], axis=0)
            for i in DEPTH_STEPS:
                remote(skip_sum, skip_parts.at[plane], 3, me, (plane + i) % DEPTH).start()
            others = skip_parts.at[pl.ds(0, DEPTH - 1)]
            wait_for(others, recv_sem.at[3])
            skip_parts[plane] = skip_sum[...]
            skip_home[...] = jnp.sum(skip_parts[...], axis=0)
            for mask in CHIP_MASKS:
                remote(skip_home, skip_home, 6, me ^ (2 * mask), plane).start()
                remote(skip_home, skip_home, 6, me ^ (2 * mask + 1), plane).start()
            remote(skip_home, skip_home, 6, me ^ 1, plane).start()
            wait_for(others, send_sem.at[3])
            wait_for(skip_in.at[pl.ds(0, PEERS - 1)], send_sem.at[6])

        wait_for(send_buf, send_sem.at[0])
        wait_for(send_taps_buf, send_sem.at[5])
        wait_for(home_buf, recv_sem.at[1])

        @pl.when(jnp.logical_not(is_hub))
        def _():
            wait_skip()

    @pl.when(is_owner)
    def _():
        pl.semaphore_wait(barrier, PEERS - 1)
        send_share()
        for mask in CHIP_MASKS:
            send_rows(mask)
        for mask in CHIP_MASKS:
            send_taps(mask)
        slab(recv_buf, me)[...] = slab(send_buf, channel)[...]
        recv_taps_buf[me] = send_taps_buf[channel]
        for load in loads[3:]:
            load.wait()
        wait_for(recv_buf.at[pl.ds(0, ROWS * (PEERS - 1))], recv_sem.at[0])

        def gather(part):
            return jnp.concatenate(
                [recv_buf[pl.ds(PIECES * part + r, PEERS, stride=ROWS), :] for r in range(PIECES)], axis=0
            )

        signal, cotangent = gather(0), gather(1)
        signal_spec = second(forward_exact(signal, table, twiddle), table)
        cot_spec = second(forward_exact(cotangent, table, twiddle), table)
        lags = inverse(product_conj(signal_spec, cot_spec), table, twiddle)
        for r in range(PIECES):
            lag_buf[:, r, :] = lags[PEERS * r : PEERS * (r + 1)]

        slot = (channel % 2) * DEPTH + plane

        def send_lags(mask):
            there = me ^ mask
            return remote(lag_buf.at[there], lag_home.at[slot], 4, there, lag_plane)

        def send_all_lags():
            pl.semaphore_wait(ready_sem, 1)
            for mask in CHIP_MASKS:
                send_lags(2 * mask).start()
                send_lags(2 * mask + 1).start()
            send_lags(1).start()

            @pl.when(in_place)
            def _():
                pltpu.make_async_copy(lag_buf.at[me], lag_home.at[slot], recv_sem.at[4]).start()

            @pl.when(jnp.logical_not(in_place))
            def _():
                send_lags(0).start()

        lags_first = jnp.logical_and(plane >= 3, plane <= 6)

        @pl.when(lags_first)
        def _():
            send_all_lags()

        wait_for(recv_taps_buf.at[pl.ds(0, PEERS - 1)], recv_sem.at[5])
        taps_rows = jnp.concatenate([recv_taps_buf[:, r, :] for r in range(PIECES)], axis=0)
        filter_spec = second(forward_full(taps_rows, table, twiddle), table)
        own_gain = gain[channel]
        conv_out = inverse(product(filter_spec, signal_spec), table, twiddle) + own_gain * signal
        conv_grad = inverse(product_conj(filter_spec, cot_spec), table, twiddle) + own_gain * cotangent
        for r in range(PIECES):
            rows = slice(PEERS * r, PEERS * (r + 1))
            back_buf[pl.ds(r, PEERS, stride=ROWS), :] = conv_out[rows]
            back_buf[pl.ds(PIECES + r, PEERS, stride=ROWS), :] = conv_grad[rows]

        def send_results(mask):
            there = me ^ mask
            remote(slab(back_buf, there), slab(home_buf, channel), 1, there, plane).start()

        for mask in CHIP_MASKS:
            send_results(2 * mask)
            send_results(2 * mask + 1)
        send_results(1)
        slab(home_buf, channel)[...] = slab(back_buf, me)[...]

        @pl.when(jnp.logical_not(lags_first))
        def _():
            send_all_lags()

        wait_for(send_buf.at[pl.ds(0, ROWS * (CHIPS - 1))], send_sem.at[0])
        wait_for(send_taps_buf.at[pl.ds(0, CHIPS - 1)], send_sem.at[5])
        wait_for(back_buf.at[pl.ds(0, ROWS * (PEERS - 1))], send_sem.at[1])
        wait_for(home_buf.at[pl.ds(0, ROWS * (CHIPS - 1))], recv_sem.at[1])
        wait_for(lag_buf.at[pl.ds(0, PEERS - 1)], send_sem.at[4])

        @pl.when(jnp.logical_not(in_place))
        def _():
            wait_for(lag_buf.at[0], send_sem.at[4])

        wait_skip()

    wait_for(lag_home, recv_sem.at[4])


def finish(home_buf, lag_home, skip_home, out_ref, grad_ref, lag_ref, skip_ref):
    for r in range(PIECES):
        lanes = slice(SIDE * r, SIDE * (r + 1))
        out_ref[:, lanes] = home_buf[pl.ds(r, CHIPS, stride=ROWS), :].astype(BF16)
        grad_ref[:, lanes] = home_buf[pl.ds(PIECES + r, CHIPS, stride=ROWS), :].astype(BF16)
    for j in range(2):
        lags = jnp.sum(lag_home[DEPTH * j : DEPTH * (j + 1)], axis=0) * SCALE
        for r in range(PIECES):
            lag_ref[j : j + 1, SIDE * r : SIDE * (r + 1)] = lags[r : r + 1]
    skip_ref[...] = skip_home[0] * SCALE


def on_device(signal, cotangent, filter_taps, skip_gain):
    square, twiddle = tables()
    anywhere = pl.BlockSpec(memory_space=pl.ANY)
    vmem = pl.BlockSpec(memory_space=pltpu.VMEM)
    operands = (signal, cotangent, filter_taps, skip_gain, jnp.asarray(square), jnp.asarray(twiddle))
    received = pl.pallas_call(
        exchange,
        out_shape=(
            pltpu.VMEM((CHIPS * ROWS, SIDE), F32),
            pltpu.VMEM((2 * DEPTH, PIECES, SIDE), F32),
            pltpu.VMEM((1, SIDE), F32),
        ),
        in_specs=[anywhere] * 6,
        out_specs=(vmem,) * 3,
        scratch_shapes=[
            pltpu.VMEM((CHIPS, LOCAL), BF16),
            pltpu.VMEM((CHIPS, LOCAL), BF16),
            pltpu.VMEM((CHIPS, LOCAL), F32),
            pltpu.SMEM((CHIPS,), F32),
            pltpu.VMEM((TABLE_ROWS, 2 * SIDE), BF16),
            pltpu.VMEM((2 * SIDE, SIDE), F32),
            pltpu.VMEM((CHIPS * ROWS, SIDE), F32),
            pltpu.VMEM((CHIPS, PIECES, SIDE), F32),
            pltpu.VMEM((PEERS * ROWS, SIDE), F32),
            pltpu.VMEM((PEERS, PIECES, SIDE), F32),
            pltpu.VMEM((PEERS * ROWS, SIDE), F32),
            pltpu.VMEM((PEERS, PIECES, SIDE), F32),
            pltpu.VMEM((1, SIDE), F32),
            pltpu.VMEM((PEERS, 1, SIDE), F32),
            pltpu.VMEM((1, SIDE), F32),
            pltpu.VMEM((DEPTH, 1, SIDE), F32),
            pltpu.SemaphoreType.DMA((6,)),
            pltpu.SemaphoreType.DMA((7,)),
            pltpu.SemaphoreType.DMA((7,)),
            pltpu.SemaphoreType.REGULAR,
            pltpu.SemaphoreType.REGULAR,
        ],
        compiler_params=pltpu.CompilerParams(
            collective_id=0, has_side_effects=True, vmem_limit_bytes=32 * 1024 * 1024
        ),
        name="exchange",
    )(*(pltpu.with_memory_space_constraint(operand, pltpu.HBM) for operand in operands))
    return pl.pallas_call(
        finish,
        out_shape=(
            jax.ShapeDtypeStruct((CHIPS, LOCAL), BF16),
            jax.ShapeDtypeStruct((CHIPS, LOCAL), BF16),
            jax.ShapeDtypeStruct((2, LOCAL), F32),
            jax.ShapeDtypeStruct((SIDE,), F32),
        ),
        in_specs=[vmem] * 3,
        out_specs=(vmem,) * 4,
        compiler_params=pltpu.CompilerParams(vmem_limit_bytes=8 * 1024 * 1024),
        name="finish",
    )(*received)


def solution(mesh):
    in_specs = (P("ch", "seq"), P("ch", "seq"), P(None, "seq"), P("ch"))
    out_specs = (P("ch", "seq"), P("ch", "seq"), P("ch", "seq"), P())
    return jax.shard_map(on_device, mesh=mesh, in_specs=in_specs, out_specs=out_specs, check_vma=False)
```

```python
import functools
import math

import jax
import jax.numpy as jnp
import ml_dtypes
import numpy as np
from jax import lax
from jax.experimental import pallas as pl
from jax.experimental.pallas import tpu as pltpu
from jax.sharding import PartitionSpec as P

MESH = pl.DeviceIdType.MESH
F32, BF16 = jnp.float32, jnp.bfloat16

CHIPS = 16
PEERS = 32
DEPTH = 8
SIDE = 128
LENGTH = SIDE * SIDE
LOCAL = 512
ROWS = 8
HUB = 1
PIECES = LOCAL // SIDE
SCALE = 1.0 / math.sqrt(LENGTH)


def hops(mask):
    return (0, 1, 2, 1)[mask & 3]


CHIP_MASKS = sorted(range(1, CHIPS), key=lambda m: -hops(m) - hops(m >> 2))
DEPTH_STEPS = sorted(range(1, DEPTH), key=lambda i: -min(i, DEPTH - i))


def split(table):
    high = table.astype(ml_dtypes.bfloat16)
    low = (table - high.astype(np.float64)).astype(ml_dtypes.bfloat16)
    return high, low


@functools.cache
def tables():
    index = np.arange(SIDE)
    row = np.arange(SIDE)
    position = PIECES * (row % PEERS) + row // PEERS
    turn = 2.0 * np.pi * np.mod(np.outer(4 * index + 1, position), 4 * SIDE) / (4 * SIDE)
    first = np.concatenate([np.cos(turn), -np.sin(turn)], axis=0)
    first_high, first_low = split(first)
    small = 2.0 * np.pi * np.mod(np.outer(index, index), SIDE) / SIDE
    cosine, sine = np.cos(small), np.sin(small)
    middle = np.block([[cosine, -sine], [sine, cosine]])
    last = np.concatenate([np.cos(turn.T), -np.sin(turn.T)], axis=1) / LENGTH
    square = np.concatenate(
        [np.concatenate([first_high, first_low], axis=1), *split(middle), *split(middle.T), *split(last)],
        axis=0,
    )
    angle = 2.0 * np.pi * np.mod(np.outer(4 * index + 1, index), 4 * LENGTH) / (4 * LENGTH)
    twiddle = np.concatenate([np.cos(angle), np.sin(angle)], axis=0).astype(np.float32)
    return square, twiddle


FIRST, MID_H, MID_L, INV_H, INV_L, LAST_H, LAST_L = 0, 256, 512, 768, 1024, 1280, 1408
TABLE_ROWS = 1536


def dot(left, right):
    return jnp.dot(left, right, preferred_element_type=F32)


def halves(value):
    high = value.astype(BF16)
    return high, (value - high.astype(F32)).astype(BF16)


def dot_right(value, table_high, table_low):
    high, low = halves(value)
    return dot(high, table_high) + (dot(low, table_high) + dot(high, table_low))


def dot_left(table_high, table_low, value):
    high, low = halves(value)
    return dot(table_high, high) + (dot(table_high, low) + dot(table_low, high))


def twist(value, twiddle):
    cosine, sine = twiddle[0:SIDE], twiddle[SIDE:]
    real, imag = value[0:SIDE], value[SIDE:]
    return jnp.concatenate([real * cosine + imag * sine, imag * cosine - real * sine], axis=1)


def untwist(value, twiddle):
    cosine, sine = twiddle[0:SIDE], twiddle[SIDE:]
    real, imag = value[:, 0:SIDE], value[:, SIDE:]
    return jnp.concatenate([real * cosine - imag * sine, imag * cosine + real * sine], axis=0)


def forward_exact(value, table, twiddle):
    high = value.astype(BF16)
    columns = dot(table[FIRST : FIRST + 256], jnp.concatenate([high, high], axis=0))
    return twist(columns, twiddle)


def forward_full(value, table, twiddle):
    high, low = halves(value)
    columns = dot(table[FIRST : FIRST + 256], jnp.concatenate([high, high], axis=0))
    columns = columns + dot(table[FIRST : FIRST + 256, 0:SIDE], low)
    return twist(columns, twiddle)


def second(value, table):
    return dot_right(value, table[MID_H : MID_H + 256], table[MID_L : MID_L + 256])


def inverse(spectrum, table, twiddle):
    columns = dot_right(spectrum, table[INV_H : INV_H + 256], table[INV_L : INV_L + 256])
    return dot_left(
        table[LAST_H : LAST_H + SIDE], table[LAST_L : LAST_L + SIDE], untwist(columns, twiddle)
    )


def product(left, right):
    a, b, c, d = left[:, :SIDE], left[:, SIDE:], right[:, :SIDE], right[:, SIDE:]
    return jnp.concatenate([a * c - b * d, a * d + b * c], axis=1)


def product_conj(left, right):
    a, b, c, d = left[:, :SIDE], left[:, SIDE:], right[:, :SIDE], right[:, SIDE:]
    return jnp.concatenate([a * c + b * d, a * d - b * c], axis=1)


def exchange(
    sig_any, cot_any, taps_any, gain_any, table_any, twiddle_any,
    home_buf, lag_home, skip_home,
    sig, cot, taps, gain, table, twiddle,
    send_buf, send_taps_buf, recv_buf, recv_taps_buf, back_buf, lag_buf, skip_row, skip_in, skip_sum, skip_parts,
    local_sem, send_sem, recv_sem, plane_sem, ready_sem,
):
    me = lax.axis_index("seq")
    plane = lax.axis_index("ch")
    chip = me // 2
    is_owner = me % 2 == 0
    is_hub = me == HUB
    shift = (PIECES - (plane & 6)) & 7

    def channel_of(p):
        return 2 * (((p >> 1) + shift) & 7) + (p & 1)

    channel = channel_of(chip)
    lag_plane = channel // 2
    in_place = lag_plane == plane
    lag_half = jnp.where((lag_plane ^ plane) < 4, 0, 1)

    loads = [
        pltpu.make_async_copy(source, target, local_sem.at[i])
        for i, (source, target) in enumerate(
            ((sig_any, sig), (cot_any, cot), (taps_any, taps), (gain_any, gain), (table_any, table), (twiddle_any, twiddle))
        )
    ]
    for load in loads[:3]:
        load.start()

    barrier = pltpu.get_barrier_semaphore()

    def greet(seq, ch):
        pl.semaphore_signal(barrier, inc=1, device_id=(seq, ch), device_id_type=MESH)

    @pl.when(jnp.logical_or(is_owner, is_hub))
    def _():
        for mask in CHIP_MASKS:
            greet(me ^ (2 * mask), plane)
            greet(me ^ (2 * mask + 1), plane)
        greet(me ^ 1, plane)

    @pl.when(is_hub)
    def _():
        for i in DEPTH_STEPS:
            greet(me, (plane + i) % DEPTH)

    @pl.when(is_owner)
    def _():
        for load in loads[3:]:
            load.start()

    @pl.when(jnp.logical_not(jnp.logical_or(is_owner, is_hub)))
    def _():
        for mask in CHIP_MASKS:
            greet(me ^ (2 * mask + 1), plane)
        greet(me ^ 1, plane)
        greet(HUB, plane)

    for load in loads[:2]:
        load.wait()
    share = jnp.sum(sig[...].astype(F32) * cot[...].astype(F32), axis=1, keepdims=True)
    lane = lax.broadcasted_iota(jnp.int32, (CHIPS, SIDE), 1)
    local = lax.broadcasted_iota(jnp.int32, (CHIPS, SIDE), 0)
    skip_row[...] = jnp.sum(jnp.where(lane == plane * CHIPS + local, share, 0.0), axis=0, keepdims=True)
    for r in range(PIECES):
        lanes = slice(SIDE * r, SIDE * (r + 1))
        send_buf[pl.ds(r, CHIPS, stride=ROWS), :] = sig[:, lanes].astype(F32)
        send_buf[pl.ds(PIECES + r, CHIPS, stride=ROWS), :] = cot[:, lanes].astype(F32)
    loads[2].wait()
    for r in range(PIECES):
        send_taps_buf[:, r, :] = taps[:, SIDE * r : SIDE * (r + 1)]

    def slab(buf, index):
        return buf.at[pl.ds(pl.multiple_of(index * ROWS, ROWS), ROWS)]

    def remote(source, target, which, seq, ch):
        return pltpu.make_async_remote_copy(
            src_ref=source, dst_ref=target, send_sem=send_sem.at[which], recv_sem=recv_sem.at[which],
            device_id=(seq, ch), device_id_type=MESH,
        )

    def wait_for(view, sem):
        pltpu.make_async_copy(view, view, sem).wait()

    def send_rows(mask):
        q = chip ^ mask
        remote(slab(send_buf, channel_of(q)), slab(recv_buf, me), 0, 2 * q, plane).start()

    def send_taps(mask):
        q = chip ^ mask
        remote(send_taps_buf.at[channel_of(q)], recv_taps_buf.at[me], 5, 2 * q, plane).start()

    def send_share():
        remote(skip_row, skip_in.at[me], 2, HUB, plane).start()

    def wait_skip():
        wait_for(skip_row, send_sem.at[2])
        wait_for(skip_home, recv_sem.at[6])

    @pl.when(jnp.logical_not(is_owner))
    def _():
        @pl.when(is_hub)
        def _():
            pl.semaphore_wait(barrier, PEERS - 1 + DEPTH - 1)
            for i in DEPTH_STEPS:
                there = (plane + i) % DEPTH
                pl.semaphore_signal(
                    plane_sem.at[jnp.where((there ^ plane) < 4, 0, 1)], inc=1, device_id=(me, there), device_id_type=MESH
                )

        @pl.when(jnp.logical_not(is_hub))
        def _():
            pl.semaphore_wait(barrier, CHIPS + 1)
            send_share()

        for mask in (*CHIP_MASKS, 0):
            send_rows(mask)
        for mask in (*CHIP_MASKS, 0):
            send_taps(mask)

        @pl.when(is_hub)
        def _():
            for half, planes in ((0, DEPTH // 2 - 1), (1, DEPTH // 2)):
                pl.semaphore_wait(plane_sem.at[half], planes)
                for mask in (*CHIP_MASKS, 0):
                    pl.semaphore_signal(
                        ready_sem.at[half], inc=1, device_id=(2 * (chip ^ mask), plane), device_id_type=MESH
                    )
            wait_for(skip_in.at[pl.ds(0, PEERS - 1)], recv_sem.at[2])
            skip_in[me] = skip_row[...]
            skip_sum[...] = jnp.sum(skip_in[...], axis=0)
            for i in DEPTH_STEPS:
                remote(skip_sum, skip_parts.at[plane], 3, me, (plane + i) % DEPTH).start()
            others = skip_parts.at[pl.ds(0, DEPTH - 1)]
            wait_for(others, recv_sem.at[3])
            skip_parts[plane] = skip_sum[...]
            skip_home[...] = jnp.sum(skip_parts[...], axis=0)
            for mask in CHIP_MASKS:
                remote(skip_home, skip_home, 6, me ^ (2 * mask), plane).start()
                remote(skip_home, skip_home, 6, me ^ (2 * mask + 1), plane).start()
            remote(skip_home, skip_home, 6, me ^ 1, plane).start()
            wait_for(others, send_sem.at[3])
            wait_for(skip_in.at[pl.ds(0, PEERS - 1)], send_sem.at[6])

        wait_for(send_buf, send_sem.at[0])
        wait_for(send_taps_buf, send_sem.at[5])
        wait_for(home_buf, recv_sem.at[1])

        @pl.when(jnp.logical_not(is_hub))
        def _():
            wait_skip()

    @pl.when(is_owner)
    def _():
        pl.semaphore_wait(barrier, PEERS - 1)
        send_share()
        for mask in CHIP_MASKS:
            send_rows(mask)
        for mask in CHIP_MASKS:
            send_taps(mask)
        slab(recv_buf, me)[...] = slab(send_buf, channel)[...]
        recv_taps_buf[me] = send_taps_buf[channel]
        for load in loads[3:]:
            load.wait()
        wait_for(recv_buf.at[pl.ds(0, ROWS * (PEERS - 1))], recv_sem.at[0])

        def gather(part):
            return jnp.concatenate(
                [recv_buf[pl.ds(PIECES * part + r, PEERS, stride=ROWS), :] for r in range(PIECES)], axis=0
            )

        signal, cotangent = gather(0), gather(1)
        signal_spec = second(forward_exact(signal, table, twiddle), table)
        cot_spec = second(forward_exact(cotangent, table, twiddle), table)
        lags = inverse(product_conj(signal_spec, cot_spec), table, twiddle)
        for r in range(PIECES):
            lag_buf[:, r, :] = lags[PEERS * r : PEERS * (r + 1)]

        slot = (channel % 2) * DEPTH + plane

        def send_lags(mask):
            there = me ^ mask
            return remote(lag_buf.at[there], lag_home.at[slot], 4, there, lag_plane)

        def send_all_lags():
            pl.semaphore_wait(ready_sem.at[lag_half], 1)
            for mask in CHIP_MASKS:
                send_lags(2 * mask).start()
                send_lags(2 * mask + 1).start()
            send_lags(1).start()

            @pl.when(in_place)
            def _():
                pltpu.make_async_copy(lag_buf.at[me], lag_home.at[slot], recv_sem.at[4]).start()

            @pl.when(jnp.logical_not(in_place))
            def _():
                send_lags(0).start()

        lags_first = plane >= 2

        @pl.when(lags_first)
        def _():
            send_all_lags()

        wait_for(recv_taps_buf.at[pl.ds(0, PEERS - 1)], recv_sem.at[5])
        taps_rows = jnp.concatenate([recv_taps_buf[:, r, :] for r in range(PIECES)], axis=0)
        filter_spec = second(forward_full(taps_rows, table, twiddle), table)
        own_gain = gain[channel]
        conv_out = inverse(product(filter_spec, signal_spec), table, twiddle) + own_gain * signal
        conv_grad = inverse(product_conj(filter_spec, cot_spec), table, twiddle) + own_gain * cotangent
        for r in range(PIECES):
            rows = slice(PEERS * r, PEERS * (r + 1))
            back_buf[pl.ds(r, PEERS, stride=ROWS), :] = conv_out[rows]
            back_buf[pl.ds(PIECES + r, PEERS, stride=ROWS), :] = conv_grad[rows]

        def send_results(mask):
            there = me ^ mask
            remote(slab(back_buf, there), slab(home_buf, channel), 1, there, plane).start()

        for mask in CHIP_MASKS:
            send_results(2 * mask)
            send_results(2 * mask + 1)
        send_results(1)
        slab(home_buf, channel)[...] = slab(back_buf, me)[...]

        @pl.when(jnp.logical_not(lags_first))
        def _():
            send_all_lags()

        wait_for(send_buf.at[pl.ds(0, ROWS * (CHIPS - 1))], send_sem.at[0])
        wait_for(send_taps_buf.at[pl.ds(0, CHIPS - 1)], send_sem.at[5])
        wait_for(back_buf.at[pl.ds(0, ROWS * (PEERS - 1))], send_sem.at[1])
        wait_for(home_buf.at[pl.ds(0, ROWS * (CHIPS - 1))], recv_sem.at[1])
        pl.semaphore_wait(ready_sem.at[1 - lag_half], 1)
        wait_for(lag_buf.at[pl.ds(0, PEERS - 1)], send_sem.at[4])

        @pl.when(jnp.logical_not(in_place))
        def _():
            wait_for(lag_buf.at[0], send_sem.at[4])

        wait_skip()

    wait_for(lag_home, recv_sem.at[4])


def finish(home_buf, lag_home, skip_home, out_ref, grad_ref, lag_ref, skip_ref):
    for r in range(PIECES):
        lanes = slice(SIDE * r, SIDE * (r + 1))
        out_ref[:, lanes] = home_buf[pl.ds(r, CHIPS, stride=ROWS), :].astype(BF16)
        grad_ref[:, lanes] = home_buf[pl.ds(PIECES + r, CHIPS, stride=ROWS), :].astype(BF16)
    for j in range(2):
        lags = jnp.sum(lag_home[DEPTH * j : DEPTH * (j + 1)], axis=0) * SCALE
        for r in range(PIECES):
            lag_ref[j : j + 1, SIDE * r : SIDE * (r + 1)] = lags[r : r + 1]
    skip_ref[...] = skip_home[0] * SCALE


def on_device(signal, cotangent, filter_taps, skip_gain):
    square, twiddle = tables()
    anywhere = pl.BlockSpec(memory_space=pl.ANY)
    vmem = pl.BlockSpec(memory_space=pltpu.VMEM)
    operands = (signal, cotangent, filter_taps, skip_gain, jnp.asarray(square), jnp.asarray(twiddle))
    received = pl.pallas_call(
        exchange,
        out_shape=(
            pltpu.VMEM((CHIPS * ROWS, SIDE), F32),
            pltpu.VMEM((2 * DEPTH, PIECES, SIDE), F32),
            pltpu.VMEM((1, SIDE), F32),
        ),
        in_specs=[anywhere] * 6,
        out_specs=(vmem,) * 3,
        scratch_shapes=[
            pltpu.VMEM((CHIPS, LOCAL), BF16),
            pltpu.VMEM((CHIPS, LOCAL), BF16),
            pltpu.VMEM((CHIPS, LOCAL), F32),
            pltpu.SMEM((CHIPS,), F32),
            pltpu.VMEM((TABLE_ROWS, 2 * SIDE), BF16),
            pltpu.VMEM((2 * SIDE, SIDE), F32),
            pltpu.VMEM((CHIPS * ROWS, SIDE), F32),
            pltpu.VMEM((CHIPS, PIECES, SIDE), F32),
            pltpu.VMEM((PEERS * ROWS, SIDE), F32),
            pltpu.VMEM((PEERS, PIECES, SIDE), F32),
            pltpu.VMEM((PEERS * ROWS, SIDE), F32),
            pltpu.VMEM((PEERS, PIECES, SIDE), F32),
            pltpu.VMEM((1, SIDE), F32),
            pltpu.VMEM((PEERS, 1, SIDE), F32),
            pltpu.VMEM((1, SIDE), F32),
            pltpu.VMEM((DEPTH, 1, SIDE), F32),
            pltpu.SemaphoreType.DMA((6,)),
            pltpu.SemaphoreType.DMA((7,)),
            pltpu.SemaphoreType.DMA((7,)),
            pltpu.SemaphoreType.REGULAR((2,)),
            pltpu.SemaphoreType.REGULAR((2,)),
        ],
        compiler_params=pltpu.CompilerParams(
            collective_id=0, has_side_effects=True, vmem_limit_bytes=32 * 1024 * 1024
        ),
        name="exchange",
    )(*(pltpu.with_memory_space_constraint(operand, pltpu.HBM) for operand in operands))
    return pl.pallas_call(
        finish,
        out_shape=(
            jax.ShapeDtypeStruct((CHIPS, LOCAL), BF16),
            jax.ShapeDtypeStruct((CHIPS, LOCAL), BF16),
            jax.ShapeDtypeStruct((2, LOCAL), F32),
            jax.ShapeDtypeStruct((SIDE,), F32),
        ),
        in_specs=[vmem] * 3,
        out_specs=(vmem,) * 4,
        compiler_params=pltpu.CompilerParams(vmem_limit_bytes=8 * 1024 * 1024),
        name="finish",
    )(*received)


def solution(mesh):
    in_specs = (P("ch", "seq"), P("ch", "seq"), P(None, "seq"), P("ch"))
    out_specs = (P("ch", "seq"), P("ch", "seq"), P("ch", "seq"), P())
    return jax.shard_map(on_device, mesh=mesh, in_specs=in_specs, out_specs=out_specs, check_vma=False)
```

```python
import functools
import math

import jax
import jax.numpy as jnp
import ml_dtypes
import numpy as np
from jax import lax
from jax.experimental import pallas as pl
from jax.experimental.pallas import tpu as pltpu
from jax.sharding import PartitionSpec as P

MESH = pl.DeviceIdType.MESH
F32, BF16 = jnp.float32, jnp.bfloat16

CHIPS = 16
PEERS = 32
DEPTH = 8
SIDE = 128
LENGTH = SIDE * SIDE
LOCAL = 512
ROWS = 8
HUB = 1
PIECES = LOCAL // SIDE
SCALE = 1.0 / math.sqrt(LENGTH)


def hops(mask):
    return (0, 1, 2, 1)[mask & 3]


CHIP_MASKS = sorted(range(1, CHIPS), key=lambda m: -hops(m) - hops(m >> 2))
DEPTH_STEPS = sorted(range(1, DEPTH), key=lambda i: -min(i, DEPTH - i))


def split(table):
    high = table.astype(ml_dtypes.bfloat16)
    low = (table - high.astype(np.float64)).astype(ml_dtypes.bfloat16)
    return high, low


@functools.cache
def tables():
    index = np.arange(SIDE)
    row = np.arange(SIDE)
    position = PIECES * (row % PEERS) + row // PEERS
    turn = 2.0 * np.pi * np.mod(np.outer(4 * index + 1, position), 4 * SIDE) / (4 * SIDE)
    first = np.concatenate([np.cos(turn), -np.sin(turn)], axis=0)
    first_high, first_low = split(first)
    small = 2.0 * np.pi * np.mod(np.outer(index, index), SIDE) / SIDE
    cosine, sine = np.cos(small), np.sin(small)
    middle = np.block([[cosine, -sine], [sine, cosine]])
    last = np.concatenate([np.cos(turn.T), -np.sin(turn.T)], axis=1) / LENGTH
    square = np.concatenate(
        [np.concatenate([first_high, first_low], axis=1), *split(middle), *split(middle.T), *split(last)],
        axis=0,
    )
    angle = 2.0 * np.pi * np.mod(np.outer(4 * index + 1, index), 4 * LENGTH) / (4 * LENGTH)
    twiddle = np.concatenate([np.cos(angle), np.sin(angle)], axis=0).astype(np.float32)
    return square, twiddle


FIRST, MID_H, MID_L, INV_H, INV_L, LAST_H, LAST_L = 0, 256, 512, 768, 1024, 1280, 1408
TABLE_ROWS = 1536


def dot(left, right):
    return jnp.dot(left, right, preferred_element_type=F32)


def halves(value):
    high = value.astype(BF16)
    return high, (value - high.astype(F32)).astype(BF16)


def dot_right(value, table_high, table_low):
    high, low = halves(value)
    return dot(high, table_high) + (dot(low, table_high) + dot(high, table_low))


def dot_left(table_high, table_low, value):
    high, low = halves(value)
    return dot(table_high, high) + (dot(table_high, low) + dot(table_low, high))


def twist(value, twiddle):
    cosine, sine = twiddle[0:SIDE], twiddle[SIDE:]
    real, imag = value[0:SIDE], value[SIDE:]
    return jnp.concatenate([real * cosine + imag * sine, imag * cosine - real * sine], axis=1)


def untwist(value, twiddle):
    cosine, sine = twiddle[0:SIDE], twiddle[SIDE:]
    real, imag = value[:, 0:SIDE], value[:, SIDE:]
    return jnp.concatenate([real * cosine - imag * sine, imag * cosine + real * sine], axis=0)


def forward_exact(value, table, twiddle):
    high = value.astype(BF16)
    columns = dot(table[FIRST : FIRST + 256], jnp.concatenate([high, high], axis=0))
    return twist(columns, twiddle)


def forward_full(value, table, twiddle):
    high, low = halves(value)
    columns = dot(table[FIRST : FIRST + 256], jnp.concatenate([high, high], axis=0))
    columns = columns + dot(table[FIRST : FIRST + 256, 0:SIDE], low)
    return twist(columns, twiddle)


def second(value, table):
    return dot_right(value, table[MID_H : MID_H + 256], table[MID_L : MID_L + 256])


def inverse(spectrum, table, twiddle):
    columns = dot_right(spectrum, table[INV_H : INV_H + 256], table[INV_L : INV_L + 256])
    return dot_left(
        table[LAST_H : LAST_H + SIDE], table[LAST_L : LAST_L + SIDE], untwist(columns, twiddle)
    )


def product(left, right):
    a, b, c, d = left[:, :SIDE], left[:, SIDE:], right[:, :SIDE], right[:, SIDE:]
    return jnp.concatenate([a * c - b * d, a * d + b * c], axis=1)


def product_conj(left, right):
    a, b, c, d = left[:, :SIDE], left[:, SIDE:], right[:, :SIDE], right[:, SIDE:]
    return jnp.concatenate([a * c + b * d, a * d - b * c], axis=1)


def exchange(
    sig_any, cot_any, taps_any, gain_any, table_any, twiddle_any,
    home_buf, lag_home, skip_home,
    sig, cot, taps, gain, table, twiddle,
    send_buf, send_taps_buf, recv_buf, recv_taps_buf, back_buf, lag_buf, skip_row, skip_in, skip_sum, skip_parts,
    local_sem, send_sem, recv_sem, plane_sem, ready_sem,
):
    me = lax.axis_index("seq")
    plane = lax.axis_index("ch")
    chip = me // 2
    is_owner = me % 2 == 0
    is_hub = me == HUB
    shift = (PIECES - (plane & 6)) & 7

    def channel_of(p):
        return 2 * (((p >> 1) + shift) & 7) + (p & 1)

    channel = channel_of(chip)
    lag_plane = channel // 2
    in_place = lag_plane == plane
    lag_half = jnp.where((lag_plane ^ plane) < 4, 0, 1)

    loads = [
        pltpu.make_async_copy(source, target, local_sem.at[i])
        for i, (source, target) in enumerate(
            ((sig_any, sig), (cot_any, cot), (taps_any, taps), (gain_any, gain), (table_any, table), (twiddle_any, twiddle))
        )
    ]
    for load in loads[:3]:
        load.start()

    barrier = pltpu.get_barrier_semaphore()

    def greet(seq, ch):
        pl.semaphore_signal(barrier, inc=1, device_id=(seq, ch), device_id_type=MESH)

    @pl.when(jnp.logical_or(is_owner, is_hub))
    def _():
        for mask in CHIP_MASKS:
            greet(me ^ (2 * mask), plane)
            greet(me ^ (2 * mask + 1), plane)
        greet(me ^ 1, plane)

    @pl.when(is_hub)
    def _():
        for i in DEPTH_STEPS:
            greet(me, (plane + i) % DEPTH)

    @pl.when(is_owner)
    def _():
        for load in loads[3:]:
            load.start()

    @pl.when(jnp.logical_not(jnp.logical_or(is_owner, is_hub)))
    def _():
        for mask in CHIP_MASKS:
            greet(me ^ (2 * mask + 1), plane)
        greet(me ^ 1, plane)
        greet(HUB, plane)

    for load in loads[:2]:
        load.wait()
    share = jnp.sum(sig[...].astype(F32) * cot[...].astype(F32), axis=1, keepdims=True)
    lane = lax.broadcasted_iota(jnp.int32, (CHIPS, SIDE), 1)
    local = lax.broadcasted_iota(jnp.int32, (CHIPS, SIDE), 0)
    skip_row[...] = jnp.sum(jnp.where(lane == plane * CHIPS + local, share, 0.0), axis=0, keepdims=True)
    for r in range(PIECES):
        lanes = slice(SIDE * r, SIDE * (r + 1))
        send_buf[pl.ds(r, CHIPS, stride=ROWS), :] = sig[:, lanes].astype(F32)
        send_buf[pl.ds(PIECES + r, CHIPS, stride=ROWS), :] = cot[:, lanes].astype(F32)
    loads[2].wait()
    for r in range(PIECES):
        send_taps_buf[:, r, :] = taps[:, SIDE * r : SIDE * (r + 1)]

    def slab(buf, index):
        return buf.at[pl.ds(pl.multiple_of(index * ROWS, ROWS), ROWS)]

    def remote(source, target, which, seq, ch):
        return pltpu.make_async_remote_copy(
            src_ref=source, dst_ref=target, send_sem=send_sem.at[which], recv_sem=recv_sem.at[which],
            device_id=(seq, ch), device_id_type=MESH,
        )

    def wait_for(view, sem):
        pltpu.make_async_copy(view, view, sem).wait()

    def send_rows(mask):
        q = chip ^ mask
        remote(slab(send_buf, channel_of(q)), slab(recv_buf, me), 0, 2 * q, plane).start()

    def send_taps(mask):
        q = chip ^ mask
        remote(send_taps_buf.at[channel_of(q)], recv_taps_buf.at[me], 5, 2 * q, plane).start()

    def send_share():
        remote(skip_row, skip_in.at[me], 2, HUB, plane).start()

    def wait_skip():
        wait_for(skip_row, send_sem.at[2])
        wait_for(skip_home, recv_sem.at[6])

    @pl.when(jnp.logical_not(is_owner))
    def _():
        @pl.when(is_hub)
        def _():
            pl.semaphore_wait(barrier, PEERS - 1 + DEPTH - 1)
            for i in DEPTH_STEPS:
                there = (plane + i) % DEPTH
                pl.semaphore_signal(
                    plane_sem.at[jnp.where((there ^ plane) < 4, 0, 1)], inc=1, device_id=(me, there), device_id_type=MESH
                )

        @pl.when(jnp.logical_not(is_hub))
        def _():
            pl.semaphore_wait(barrier, CHIPS + 1)
            send_share()

        for mask in (*CHIP_MASKS, 0):
            send_rows(mask)
        for mask in (*CHIP_MASKS, 0):
            send_taps(mask)

        @pl.when(is_hub)
        def _():
            for half, planes in ((0, DEPTH // 2 - 1), (1, DEPTH // 2)):
                pl.semaphore_wait(plane_sem.at[half], planes)
                for mask in (*CHIP_MASKS, 0):
                    pl.semaphore_signal(
                        ready_sem.at[half], inc=1, device_id=(2 * (chip ^ mask), plane), device_id_type=MESH
                    )
            wait_for(skip_in.at[pl.ds(0, PEERS - 1)], recv_sem.at[2])
            skip_in[me] = skip_row[...]
            skip_sum[...] = jnp.sum(skip_in[...], axis=0)
            for i in DEPTH_STEPS:
                remote(skip_sum, skip_parts.at[plane], 3, me, (plane + i) % DEPTH).start()
            others = skip_parts.at[pl.ds(0, DEPTH - 1)]
            wait_for(others, recv_sem.at[3])
            skip_parts[plane] = skip_sum[...]
            skip_home[...] = jnp.sum(skip_parts[...], axis=0)
            for mask in CHIP_MASKS:
                remote(skip_home, skip_home, 6, me ^ (2 * mask), plane).start()
                remote(skip_home, skip_home, 6, me ^ (2 * mask + 1), plane).start()
            remote(skip_home, skip_home, 6, me ^ 1, plane).start()
            wait_for(others, send_sem.at[3])
            wait_for(skip_in.at[pl.ds(0, PEERS - 1)], send_sem.at[6])

        wait_for(send_buf, send_sem.at[0])
        wait_for(send_taps_buf, send_sem.at[5])
        wait_for(home_buf, recv_sem.at[1])

        @pl.when(jnp.logical_not(is_hub))
        def _():
            wait_skip()

    @pl.when(is_owner)
    def _():
        pl.semaphore_wait(barrier, PEERS - 1)
        send_share()
        for mask in CHIP_MASKS:
            send_rows(mask)
        for mask in CHIP_MASKS:
            send_taps(mask)
        slab(recv_buf, me)[...] = slab(send_buf, channel)[...]
        recv_taps_buf[me] = send_taps_buf[channel]
        for load in loads[3:]:
            load.wait()
        wait_for(recv_buf.at[pl.ds(0, ROWS * (PEERS - 1))], recv_sem.at[0])

        def gather(part):
            return jnp.concatenate(
                [recv_buf[pl.ds(PIECES * part + r, PEERS, stride=ROWS), :] for r in range(PIECES)], axis=0
            )

        signal, cotangent = gather(0), gather(1)
        signal_spec = second(forward_exact(signal, table, twiddle), table)
        cot_spec = second(forward_exact(cotangent, table, twiddle), table)
        lags = inverse(product_conj(signal_spec, cot_spec), table, twiddle)
        for r in range(PIECES):
            lag_buf[:, r, :] = lags[PEERS * r : PEERS * (r + 1)]

        slot = (channel % 2) * DEPTH + plane

        def send_lags(there):
            return remote(lag_buf.at[there], lag_home.at[slot], 4, there, lag_plane)

        def send_all_lags():
            pl.semaphore_wait(ready_sem.at[lag_half], 1)

            for target in (0, *reversed(CHIP_MASKS)):
                own = jnp.logical_and(in_place, chip == target)

                @pl.when(jnp.logical_not(own))
                def _():
                    send_lags(2 * target).start()

                @pl.when(own)
                def _():
                    pltpu.make_async_copy(lag_buf.at[me], lag_home.at[slot], recv_sem.at[4]).start()

                send_lags(2 * target + 1).start()

        lags_first = plane >= 2

        @pl.when(lags_first)
        def _():
            send_all_lags()

        wait_for(recv_taps_buf.at[pl.ds(0, PEERS - 1)], recv_sem.at[5])
        taps_rows = jnp.concatenate([recv_taps_buf[:, r, :] for r in range(PIECES)], axis=0)
        filter_spec = second(forward_full(taps_rows, table, twiddle), table)
        own_gain = gain[channel]
        conv_out = inverse(product(filter_spec, signal_spec), table, twiddle) + own_gain * signal
        conv_grad = inverse(product_conj(filter_spec, cot_spec), table, twiddle) + own_gain * cotangent
        for r in range(PIECES):
            rows = slice(PEERS * r, PEERS * (r + 1))
            back_buf[pl.ds(r, PEERS, stride=ROWS), :] = conv_out[rows]
            back_buf[pl.ds(PIECES + r, PEERS, stride=ROWS), :] = conv_grad[rows]

        def send_results(mask):
            there = me ^ mask
            remote(slab(back_buf, there), slab(home_buf, channel), 1, there, plane).start()

        for mask in CHIP_MASKS:
            send_results(2 * mask)
            send_results(2 * mask + 1)
        send_results(1)
        slab(home_buf, channel)[...] = slab(back_buf, me)[...]

        @pl.when(jnp.logical_not(lags_first))
        def _():
            send_all_lags()

        wait_for(send_buf.at[pl.ds(0, ROWS * (CHIPS - 1))], send_sem.at[0])
        wait_for(send_taps_buf.at[pl.ds(0, CHIPS - 1)], send_sem.at[5])
        wait_for(back_buf.at[pl.ds(0, ROWS * (PEERS - 1))], send_sem.at[1])
        wait_for(home_buf.at[pl.ds(0, ROWS * (CHIPS - 1))], recv_sem.at[1])
        pl.semaphore_wait(ready_sem.at[1 - lag_half], 1)
        wait_for(lag_buf.at[pl.ds(0, PEERS - 1)], send_sem.at[4])

        @pl.when(jnp.logical_not(in_place))
        def _():
            wait_for(lag_buf.at[0], send_sem.at[4])

        wait_skip()

    wait_for(lag_home, recv_sem.at[4])


def finish(home_buf, lag_home, skip_home, out_ref, grad_ref, lag_ref, skip_ref):
    for r in range(PIECES):
        lanes = slice(SIDE * r, SIDE * (r + 1))
        out_ref[:, lanes] = home_buf[pl.ds(r, CHIPS, stride=ROWS), :].astype(BF16)
        grad_ref[:, lanes] = home_buf[pl.ds(PIECES + r, CHIPS, stride=ROWS), :].astype(BF16)
    for j in range(2):
        lags = jnp.sum(lag_home[DEPTH * j : DEPTH * (j + 1)], axis=0) * SCALE
        for r in range(PIECES):
            lag_ref[j : j + 1, SIDE * r : SIDE * (r + 1)] = lags[r : r + 1]
    skip_ref[...] = skip_home[0] * SCALE


def on_device(signal, cotangent, filter_taps, skip_gain):
    square, twiddle = tables()
    anywhere = pl.BlockSpec(memory_space=pl.ANY)
    vmem = pl.BlockSpec(memory_space=pltpu.VMEM)
    operands = (signal, cotangent, filter_taps, skip_gain, jnp.asarray(square), jnp.asarray(twiddle))
    received = pl.pallas_call(
        exchange,
        out_shape=(
            pltpu.VMEM((CHIPS * ROWS, SIDE), F32),
            pltpu.VMEM((2 * DEPTH, PIECES, SIDE), F32),
            pltpu.VMEM((1, SIDE), F32),
        ),
        in_specs=[anywhere] * 6,
        out_specs=(vmem,) * 3,
        scratch_shapes=[
            pltpu.VMEM((CHIPS, LOCAL), BF16),
            pltpu.VMEM((CHIPS, LOCAL), BF16),
            pltpu.VMEM((CHIPS, LOCAL), F32),
            pltpu.SMEM((CHIPS,), F32),
            pltpu.VMEM((TABLE_ROWS, 2 * SIDE), BF16),
            pltpu.VMEM((2 * SIDE, SIDE), F32),
            pltpu.VMEM((CHIPS * ROWS, SIDE), F32),
            pltpu.VMEM((CHIPS, PIECES, SIDE), F32),
            pltpu.VMEM((PEERS * ROWS, SIDE), F32),
            pltpu.VMEM((PEERS, PIECES, SIDE), F32),
            pltpu.VMEM((PEERS * ROWS, SIDE), F32),
            pltpu.VMEM((PEERS, PIECES, SIDE), F32),
            pltpu.VMEM((1, SIDE), F32),
            pltpu.VMEM((PEERS, 1, SIDE), F32),
            pltpu.VMEM((1, SIDE), F32),
            pltpu.VMEM((DEPTH, 1, SIDE), F32),
            pltpu.SemaphoreType.DMA((6,)),
            pltpu.SemaphoreType.DMA((7,)),
            pltpu.SemaphoreType.DMA((7,)),
            pltpu.SemaphoreType.REGULAR((2,)),
            pltpu.SemaphoreType.REGULAR((2,)),
        ],
        compiler_params=pltpu.CompilerParams(
            collective_id=0, has_side_effects=True, vmem_limit_bytes=32 * 1024 * 1024
        ),
        name="exchange",
    )(*(pltpu.with_memory_space_constraint(operand, pltpu.HBM) for operand in operands))
    return pl.pallas_call(
        finish,
        out_shape=(
            jax.ShapeDtypeStruct((CHIPS, LOCAL), BF16),
            jax.ShapeDtypeStruct((CHIPS, LOCAL), BF16),
            jax.ShapeDtypeStruct((2, LOCAL), F32),
            jax.ShapeDtypeStruct((SIDE,), F32),
        ),
        in_specs=[vmem] * 3,
        out_specs=(vmem,) * 4,
        compiler_params=pltpu.CompilerParams(vmem_limit_bytes=8 * 1024 * 1024),
        name="finish",
    )(*received)


def solution(mesh):
    in_specs = (P("ch", "seq"), P("ch", "seq"), P(None, "seq"), P("ch"))
    out_specs = (P("ch", "seq"), P("ch", "seq"), P("ch", "seq"), P())
    return jax.shard_map(on_device, mesh=mesh, in_specs=in_specs, out_specs=out_specs, check_vma=False)
```

```python
import functools
import math

import jax
import jax.numpy as jnp
import ml_dtypes
import numpy as np
from jax import lax
from jax.experimental import pallas as pl
from jax.experimental.pallas import tpu as pltpu
from jax.sharding import PartitionSpec as P

MESH = pl.DeviceIdType.MESH
F32, BF16 = jnp.float32, jnp.bfloat16

CHIPS = 16
PEERS = 32
DEPTH = 8
SIDE = 128
LENGTH = SIDE * SIDE
LOCAL = 512
ROWS = 8
HUB = 1
PIECES = LOCAL // SIDE
SCALE = 1.0 / math.sqrt(LENGTH)


def hops(mask):
    return (0, 1, 2, 1)[mask & 3]


CHIP_MASKS = sorted(range(1, CHIPS), key=lambda m: -hops(m) - hops(m >> 2))
DEPTH_STEPS = sorted(range(1, DEPTH), key=lambda i: -min(i, DEPTH - i))


def split(table):
    high = table.astype(ml_dtypes.bfloat16)
    low = (table - high.astype(np.float64)).astype(ml_dtypes.bfloat16)
    return high, low


@functools.cache
def tables():
    index = np.arange(SIDE)
    row = np.arange(SIDE)
    position = PIECES * (row % PEERS) + row // PEERS
    turn = 2.0 * np.pi * np.mod(np.outer(4 * index + 1, position), 4 * SIDE) / (4 * SIDE)
    first = np.concatenate([np.cos(turn), -np.sin(turn)], axis=0)
    first_high, first_low = split(first)
    small = 2.0 * np.pi * np.mod(np.outer(index, index), SIDE) / SIDE
    cosine, sine = np.cos(small), np.sin(small)
    middle = np.block([[cosine, -sine], [sine, cosine]])
    last = np.concatenate([np.cos(turn.T), -np.sin(turn.T)], axis=1) / LENGTH
    square = np.concatenate(
        [np.concatenate([first_high, first_low], axis=1), *split(middle), *split(middle.T), *split(last)],
        axis=0,
    )
    angle = 2.0 * np.pi * np.mod(np.outer(4 * index + 1, index), 4 * LENGTH) / (4 * LENGTH)
    twiddle = np.concatenate([np.cos(angle), np.sin(angle)], axis=0).astype(np.float32)
    return square, twiddle


FIRST, MID_H, MID_L, INV_H, INV_L, LAST_H, LAST_L = 0, 256, 512, 768, 1024, 1280, 1408
TABLE_ROWS = 1536


def dot(left, right):
    return jnp.dot(left, right, preferred_element_type=F32)


def halves(value):
    high = value.astype(BF16)
    return high, (value - high.astype(F32)).astype(BF16)


def dot_right(value, table_high, table_low):
    high, low = halves(value)
    return dot(high, table_high) + (dot(low, table_high) + dot(high, table_low))


def dot_left(table_high, table_low, value):
    high, low = halves(value)
    return dot(table_high, high) + (dot(table_high, low) + dot(table_low, high))


def twist(value, twiddle):
    cosine, sine = twiddle[0:SIDE], twiddle[SIDE:]
    real, imag = value[0:SIDE], value[SIDE:]
    return jnp.concatenate([real * cosine + imag * sine, imag * cosine - real * sine], axis=1)


def untwist(value, twiddle):
    cosine, sine = twiddle[0:SIDE], twiddle[SIDE:]
    real, imag = value[:, 0:SIDE], value[:, SIDE:]
    return jnp.concatenate([real * cosine - imag * sine, imag * cosine + real * sine], axis=0)


def forward_exact(value, table, twiddle):
    high = value.astype(BF16)
    columns = dot(table[FIRST : FIRST + 256], jnp.concatenate([high, high], axis=0))
    return twist(columns, twiddle)


def forward_full(value, table, twiddle):
    high, low = halves(value)
    columns = dot(table[FIRST : FIRST + 256], jnp.concatenate([high, high], axis=0))
    columns = columns + dot(table[FIRST : FIRST + 256, 0:SIDE], low)
    return twist(columns, twiddle)


def second(value, table):
    return dot_right(value, table[MID_H : MID_H + 256], table[MID_L : MID_L + 256])


def inverse(spectrum, table, twiddle):
    columns = dot_right(spectrum, table[INV_H : INV_H + 256], table[INV_L : INV_L + 256])
    return dot_left(
        table[LAST_H : LAST_H + SIDE], table[LAST_L : LAST_L + SIDE], untwist(columns, twiddle)
    )


def product(left, right):
    a, b, c, d = left[:, :SIDE], left[:, SIDE:], right[:, :SIDE], right[:, SIDE:]
    return jnp.concatenate([a * c - b * d, a * d + b * c], axis=1)


def product_conj(left, right):
    a, b, c, d = left[:, :SIDE], left[:, SIDE:], right[:, :SIDE], right[:, SIDE:]
    return jnp.concatenate([a * c + b * d, a * d - b * c], axis=1)


def exchange(
    sig_any, cot_any, taps_any, gain_any, table_any, twiddle_any,
    home_buf, lag_home, skip_home,
    sig, cot, taps, gain, table, twiddle,
    send_buf, send_taps_buf, recv_buf, recv_taps_buf, back_buf, lag_buf, skip_row, skip_in, skip_sum, skip_parts,
    local_sem, send_sem, recv_sem, plane_sem, ready_sem,
):
    me = lax.axis_index("seq")
    plane = lax.axis_index("ch")
    chip = me // 2
    is_owner = me % 2 == 0
    is_hub = me == HUB
    shift = (PIECES - (plane & 6)) & 7

    def channel_of(p):
        return 2 * (((p >> 1) + shift) & 7) + (p & 1)

    channel = channel_of(chip)
    lag_plane = channel // 2
    in_place = lag_plane == plane
    lag_half = jnp.where((lag_plane ^ plane) < 4, 0, 1)

    loads = [
        pltpu.make_async_copy(source, target, local_sem.at[i])
        for i, (source, target) in enumerate(
            ((sig_any, sig), (cot_any, cot), (taps_any, taps), (gain_any, gain), (table_any, table), (twiddle_any, twiddle))
        )
    ]
    for load in loads[:3]:
        load.start()

    barrier = pltpu.get_barrier_semaphore()

    def greet(seq, ch):
        pl.semaphore_signal(barrier, inc=1, device_id=(seq, ch), device_id_type=MESH)

    @pl.when(jnp.logical_or(is_owner, is_hub))
    def _():
        for mask in CHIP_MASKS:
            greet(me ^ (2 * mask), plane)
            greet(me ^ (2 * mask + 1), plane)
        greet(me ^ 1, plane)

    @pl.when(is_hub)
    def _():
        for i in DEPTH_STEPS:
            greet(me, (plane + i) % DEPTH)

    @pl.when(is_owner)
    def _():
        for load in loads[3:]:
            load.start()

    @pl.when(jnp.logical_not(jnp.logical_or(is_owner, is_hub)))
    def _():
        for mask in CHIP_MASKS:
            greet(me ^ (2 * mask + 1), plane)
        greet(me ^ 1, plane)
        greet(HUB, plane)

    for load in loads[:2]:
        load.wait()
    for r in range(PIECES):
        lanes = slice(SIDE * r, SIDE * (r + 1))
        send_buf[pl.ds(r, CHIPS, stride=ROWS), :] = sig[:, lanes].astype(F32)
        send_buf[pl.ds(PIECES + r, CHIPS, stride=ROWS), :] = cot[:, lanes].astype(F32)

    def stage_taps():
        loads[2].wait()
        for r in range(PIECES):
            send_taps_buf[:, r, :] = taps[:, SIDE * r : SIDE * (r + 1)]

    def form_share():
        share = jnp.sum(sig[...].astype(F32) * cot[...].astype(F32), axis=1, keepdims=True)
        lane = lax.broadcasted_iota(jnp.int32, (CHIPS, SIDE), 1)
        local = lax.broadcasted_iota(jnp.int32, (CHIPS, SIDE), 0)
        skip_row[...] = jnp.sum(jnp.where(lane == plane * CHIPS + local, share, 0.0), axis=0, keepdims=True)

    def slab(buf, index):
        return buf.at[pl.ds(pl.multiple_of(index * ROWS, ROWS), ROWS)]

    def remote(source, target, which, seq, ch):
        return pltpu.make_async_remote_copy(
            src_ref=source, dst_ref=target, send_sem=send_sem.at[which], recv_sem=recv_sem.at[which],
            device_id=(seq, ch), device_id_type=MESH,
        )

    def wait_for(view, sem):
        pltpu.make_async_copy(view, view, sem).wait()

    def send_rows(mask):
        q = chip ^ mask
        remote(slab(send_buf, channel_of(q)), slab(recv_buf, me), 0, 2 * q, plane).start()

    def send_taps(mask):
        q = chip ^ mask
        remote(send_taps_buf.at[channel_of(q)], recv_taps_buf.at[me], 5, 2 * q, plane).start()

    def send_share():
        remote(skip_row, skip_in.at[me], 2, HUB, plane).start()

    def wait_skip():
        wait_for(skip_row, send_sem.at[2])
        wait_for(skip_home, recv_sem.at[6])

    @pl.when(jnp.logical_not(is_owner))
    def _():
        @pl.when(is_hub)
        def _():
            pl.semaphore_wait(barrier, PEERS - 1 + DEPTH - 1)
            for i in DEPTH_STEPS:
                there = (plane + i) % DEPTH
                pl.semaphore_signal(
                    plane_sem.at[jnp.where((there ^ plane) < 4, 0, 1)], inc=1, device_id=(me, there), device_id_type=MESH
                )

        @pl.when(jnp.logical_not(is_hub))
        def _():
            pl.semaphore_wait(barrier, CHIPS + 1)

        for mask in (*CHIP_MASKS, 0):
            send_rows(mask)
        form_share()

        @pl.when(jnp.logical_not(is_hub))
        def _():
            send_share()

        stage_taps()
        for mask in (*CHIP_MASKS, 0):
            send_taps(mask)

        @pl.when(is_hub)
        def _():
            for half, planes in ((0, DEPTH // 2 - 1), (1, DEPTH // 2)):
                pl.semaphore_wait(plane_sem.at[half], planes)
                for mask in (*CHIP_MASKS, 0):
                    pl.semaphore_signal(
                        ready_sem.at[half], inc=1, device_id=(2 * (chip ^ mask), plane), device_id_type=MESH
                    )
            wait_for(skip_in.at[pl.ds(0, PEERS - 1)], recv_sem.at[2])
            skip_in[me] = skip_row[...]
            skip_sum[...] = jnp.sum(skip_in[...], axis=0)
            for i in DEPTH_STEPS:
                remote(skip_sum, skip_parts.at[plane], 3, me, (plane + i) % DEPTH).start()
            others = skip_parts.at[pl.ds(0, DEPTH - 1)]
            wait_for(others, recv_sem.at[3])
            skip_parts[plane] = skip_sum[...]
            skip_home[...] = jnp.sum(skip_parts[...], axis=0)
            for mask in CHIP_MASKS:
                remote(skip_home, skip_home, 6, me ^ (2 * mask), plane).start()
                remote(skip_home, skip_home, 6, me ^ (2 * mask + 1), plane).start()
            remote(skip_home, skip_home, 6, me ^ 1, plane).start()
            wait_for(others, send_sem.at[3])
            wait_for(skip_in.at[pl.ds(0, PEERS - 1)], send_sem.at[6])

        wait_for(send_buf, send_sem.at[0])
        wait_for(send_taps_buf, send_sem.at[5])
        wait_for(home_buf, recv_sem.at[1])

        @pl.when(jnp.logical_not(is_hub))
        def _():
            wait_skip()

    @pl.when(is_owner)
    def _():
        pl.semaphore_wait(barrier, PEERS - 1)
        for mask in CHIP_MASKS:
            send_rows(mask)
        form_share()
        send_share()
        stage_taps()
        for mask in CHIP_MASKS:
            send_taps(mask)
        slab(recv_buf, me)[...] = slab(send_buf, channel)[...]
        recv_taps_buf[me] = send_taps_buf[channel]
        for load in loads[3:]:
            load.wait()
        wait_for(recv_buf.at[pl.ds(0, ROWS * (PEERS - 1))], recv_sem.at[0])

        def gather(part):
            return jnp.concatenate(
                [recv_buf[pl.ds(PIECES * part + r, PEERS, stride=ROWS), :] for r in range(PIECES)], axis=0
            )

        signal, cotangent = gather(0), gather(1)
        signal_spec = second(forward_exact(signal, table, twiddle), table)
        cot_spec = second(forward_exact(cotangent, table, twiddle), table)
        lags = inverse(product_conj(signal_spec, cot_spec), table, twiddle)
        for r in range(PIECES):
            lag_buf[:, r, :] = lags[PEERS * r : PEERS * (r + 1)]

        slot = (channel % 2) * DEPTH + plane

        def send_lags(there):
            return remote(lag_buf.at[there], lag_home.at[slot], 4, there, lag_plane)

        def send_all_lags():
            pl.semaphore_wait(ready_sem.at[lag_half], 1)

            for target in (0, *reversed(CHIP_MASKS)):
                own = jnp.logical_and(in_place, chip == target)

                @pl.when(jnp.logical_not(own))
                def _():
                    send_lags(2 * target).start()

                @pl.when(own)
                def _():
                    pltpu.make_async_copy(lag_buf.at[me], lag_home.at[slot], recv_sem.at[4]).start()

                send_lags(2 * target + 1).start()

        lags_first = plane >= 2

        @pl.when(lags_first)
        def _():
            send_all_lags()

        wait_for(recv_taps_buf.at[pl.ds(0, PEERS - 1)], recv_sem.at[5])
        taps_rows = jnp.concatenate([recv_taps_buf[:, r, :] for r in range(PIECES)], axis=0)
        filter_spec = second(forward_full(taps_rows, table, twiddle), table)
        own_gain = gain[channel]
        conv_out = inverse(product(filter_spec, signal_spec), table, twiddle) + own_gain * signal
        conv_grad = inverse(product_conj(filter_spec, cot_spec), table, twiddle) + own_gain * cotangent
        for r in range(PIECES):
            rows = slice(PEERS * r, PEERS * (r + 1))
            back_buf[pl.ds(r, PEERS, stride=ROWS), :] = conv_out[rows]
            back_buf[pl.ds(PIECES + r, PEERS, stride=ROWS), :] = conv_grad[rows]

        def send_results(mask):
            there = me ^ mask
            remote(slab(back_buf, there), slab(home_buf, channel), 1, there, plane).start()

        for mask in CHIP_MASKS:
            send_results(2 * mask)
            send_results(2 * mask + 1)
        send_results(1)
        slab(home_buf, channel)[...] = slab(back_buf, me)[...]

        @pl.when(jnp.logical_not(lags_first))
        def _():
            send_all_lags()

        wait_for(send_buf.at[pl.ds(0, ROWS * (CHIPS - 1))], send_sem.at[0])
        wait_for(send_taps_buf.at[pl.ds(0, CHIPS - 1)], send_sem.at[5])
        wait_for(back_buf.at[pl.ds(0, ROWS * (PEERS - 1))], send_sem.at[1])
        wait_for(home_buf.at[pl.ds(0, ROWS * (CHIPS - 1))], recv_sem.at[1])
        pl.semaphore_wait(ready_sem.at[1 - lag_half], 1)
        wait_for(lag_buf.at[pl.ds(0, PEERS - 1)], send_sem.at[4])

        @pl.when(jnp.logical_not(in_place))
        def _():
            wait_for(lag_buf.at[0], send_sem.at[4])

        wait_skip()

    wait_for(lag_home, recv_sem.at[4])


def finish(home_buf, lag_home, skip_home, out_ref, grad_ref, lag_ref, skip_ref):
    for r in range(PIECES):
        lanes = slice(SIDE * r, SIDE * (r + 1))
        out_ref[:, lanes] = home_buf[pl.ds(r, CHIPS, stride=ROWS), :].astype(BF16)
        grad_ref[:, lanes] = home_buf[pl.ds(PIECES + r, CHIPS, stride=ROWS), :].astype(BF16)
    for j in range(2):
        lags = jnp.sum(lag_home[DEPTH * j : DEPTH * (j + 1)], axis=0) * SCALE
        for r in range(PIECES):
            lag_ref[j : j + 1, SIDE * r : SIDE * (r + 1)] = lags[r : r + 1]
    skip_ref[...] = skip_home[0] * SCALE


def on_device(signal, cotangent, filter_taps, skip_gain):
    square, twiddle = tables()
    anywhere = pl.BlockSpec(memory_space=pl.ANY)
    vmem = pl.BlockSpec(memory_space=pltpu.VMEM)
    operands = (signal, cotangent, filter_taps, skip_gain, jnp.asarray(square), jnp.asarray(twiddle))
    received = pl.pallas_call(
        exchange,
        out_shape=(
            pltpu.VMEM((CHIPS * ROWS, SIDE), F32),
            pltpu.VMEM((2 * DEPTH, PIECES, SIDE), F32),
            pltpu.VMEM((1, SIDE), F32),
        ),
        in_specs=[anywhere] * 6,
        out_specs=(vmem,) * 3,
        scratch_shapes=[
            pltpu.VMEM((CHIPS, LOCAL), BF16),
            pltpu.VMEM((CHIPS, LOCAL), BF16),
            pltpu.VMEM((CHIPS, LOCAL), F32),
            pltpu.SMEM((CHIPS,), F32),
            pltpu.VMEM((TABLE_ROWS, 2 * SIDE), BF16),
            pltpu.VMEM((2 * SIDE, SIDE), F32),
            pltpu.VMEM((CHIPS * ROWS, SIDE), F32),
            pltpu.VMEM((CHIPS, PIECES, SIDE), F32),
            pltpu.VMEM((PEERS * ROWS, SIDE), F32),
            pltpu.VMEM((PEERS, PIECES, SIDE), F32),
            pltpu.VMEM((PEERS * ROWS, SIDE), F32),
            pltpu.VMEM((PEERS, PIECES, SIDE), F32),
            pltpu.VMEM((1, SIDE), F32),
            pltpu.VMEM((PEERS, 1, SIDE), F32),
            pltpu.VMEM((1, SIDE), F32),
            pltpu.VMEM((DEPTH, 1, SIDE), F32),
            pltpu.SemaphoreType.DMA((6,)),
            pltpu.SemaphoreType.DMA((7,)),
            pltpu.SemaphoreType.DMA((7,)),
            pltpu.SemaphoreType.REGULAR((2,)),
            pltpu.SemaphoreType.REGULAR((2,)),
        ],
        compiler_params=pltpu.CompilerParams(
            collective_id=0, has_side_effects=True, vmem_limit_bytes=32 * 1024 * 1024
        ),
        name="exchange",
    )(*(pltpu.with_memory_space_constraint(operand, pltpu.HBM) for operand in operands))
    return pl.pallas_call(
        finish,
        out_shape=(
            jax.ShapeDtypeStruct((CHIPS, LOCAL), BF16),
            jax.ShapeDtypeStruct((CHIPS, LOCAL), BF16),
            jax.ShapeDtypeStruct((2, LOCAL), F32),
            jax.ShapeDtypeStruct((SIDE,), F32),
        ),
        in_specs=[vmem] * 3,
        out_specs=(vmem,) * 4,
        compiler_params=pltpu.CompilerParams(vmem_limit_bytes=8 * 1024 * 1024),
        name="finish",
    )(*received)


def solution(mesh):
    in_specs = (P("ch", "seq"), P("ch", "seq"), P(None, "seq"), P("ch"))
    out_specs = (P("ch", "seq"), P("ch", "seq"), P("ch", "seq"), P())
    return jax.shard_map(on_device, mesh=mesh, in_specs=in_specs, out_specs=out_specs, check_vma=False)
```
